32 devices in a mesh: src: 16 (over z, y, x), inst: 2 (over core).
Axes of the slice: x: 2, y: 2, z: 4, core: 2. Of those that a mesh axis runs over, the one named last changes fastest.
Arguments:
- observed: float32 [60, 16384], P(None, ('src', 'inst')), may hold values from -18 to 18
- basis: float32 [60, 55], replicated, may hold values from -0.875 to 0.875
- taps: float32 [9], replicated, may hold values from 0.05 to 0.35
- epoch_owner: int32 [16384, 1], P(('src', 'inst')), may hold values from 0 to 15; in each aligned block of 512 rows (0 to 511, 512 to 1023, ...) at most 48 rows name the same one
- epoch_source: int32 [16384], P(('src', 'inst')), may hold values from 0 to 4095
- epoch_config: int32 [16384], P(('src', 'inst')), may hold values from 0 to 31
- epoch_counts: int32 [32], P(('src', 'inst')), may hold values from 256 to 512, as said below
Outputs:
- solution_coeffs: float32 [55, 65536], P(None, 'src')
- solution_table: float32 [60, 32], P(None, 'inst')
- direction_coeffs: float32 [55, 65536], P(None, 'src')
- direction_table: float32 [60, 32], P(None, 'inst')
The draws below stay inside these ranges and needn't reach their ends.
Inputs may be any that keep to these rules, and one draw needn't show every extreme that they name: `epoch_owner`: among the 512 epochs of one device, at most 48 name any one owner. The first epoch_counts[d] of device d's 512 epoch slots are live.
All inputs are finite; a program needn't handle non-finite values.
Results may differ from the reference program's by a relative error of at most 0.0003.
Values sent between devices are 32-bit elements; how exact they have to be, the bound alone decides.
A program may use at most 64 MiB of HBM per device.

```python
import math
import jax
import jax.numpy as jnp
import numpy as np
from jax import lax

SAMPLES = 60
NCOEF = 55
TAPS = 9
ITERS = 2
EPD = 512
SRC_DEV = 4096
CAP = 48
SHARDS = 32
EPOCHS = 16384
SOURCES = 65536
CONFIGS = 32
N_SRC = 16


def draw_observed(key, part):
    cols = jnp.arange(EPOCHS, dtype=jnp.float32)
    rising = 1.0 + 2.0 * cols / EPOCHS
    values = jnp.clip(jax.random.normal(key, (SAMPLES, EPOCHS), jnp.float32), -6.0, 6.0)
    return values * rising[None, :]


def draw_epoch_counts(key, part):
    first, second = jax.random.split(key, 2)
    base = jax.random.randint(first, (SHARDS,), EPD // 2, EPD + 1)
    fullest = jax.random.randint(second, (), 0, SHARDS)
    return jnp.where(jnp.arange(SHARDS) == fullest, EPD, base).astype(jnp.int32)


def set_ends(array, own_key, smallest, high):
    index_at = [jax.random.randint(jax.random.fold_in(own_key, axis), (), 0, length) for axis, length in enumerate(array.shape)]
    longest = array.shape.index(max(array.shape))
    neighbour = index_at[:longest] + [(index_at[longest] + 1) % array.shape[longest]] + index_at[longest + 1:]
    return array.at[tuple(index_at)].set(smallest).at[tuple(neighbour)].set(high)


def assign_block(key, own, number, rows, count, top, most, skew):
    order = jax.random.permutation(key, count)
    crowded, usual = shares(count, rows * top, most, skew, True), shares(count, rows * top, most, skew, False)
    places = jnp.arange(count)

    def named(sizes, rotation):
        used = int((sizes > 0).sum())
        fixed = max(1, used // 4)
        shifted = fixed + (places - fixed + rotation * (used - fixed)) % max(1, count - fixed)
        return jnp.zeros((count,), jnp.int32).at[order[jnp.where(places < fixed, places, shifted)]].set(jnp.asarray(sizes, jnp.int32))

    sizes = jnp.where(number % 4 == 0, named(crowded, number // 4), named(usual, number - number // 4 - 1))
    mixed = jax.random.permutation(jax.random.fold_in(own, 3), count)
    donor, sink = mixed[0:count // 2 * 2:2], mixed[1:count // 2 * 2:2]
    slack = jnp.minimum(sizes[donor] - 1, most - sizes[sink]) // 2
    slack = jnp.where((donor == order[0]) | (sink == order[0]) | (sizes[sink] == 0), 0, jnp.maximum(slack, 0))
    shifted = jax.random.randint(jax.random.fold_in(own, 4), (count // 2,), 0, 1 << 20) % (slack + 1)
    sizes = sizes.at[donor].add(-shifted).at[sink].add(shifted)
    items = jnp.searchsorted(jnp.cumsum(sizes), jnp.arange(rows * top), side="right").astype(jnp.int32)
    listing = items.reshape(top, rows).T
    listing = listing[jax.random.permutation(jax.random.fold_in(own, 1), rows)]
    rotation = jax.random.randint(jax.random.fold_in(own, 2), (rows, 1), 0, top)
    return jnp.take_along_axis(listing, (jnp.arange(top)[None, :] + rotation) % top, axis=1)


def shares(amount, total, limit, skew, full):
    portions = [(1 << 20) // math.isqrt(grade ** skew) + 1 for grade in range(1, amount + 1)]
    largest = limit if full else min(limit, max(-(-total // amount), total * portions[0] // sum(portions)))
    least = 1 if total - largest >= amount - 1 else 0
    holding, spare = [largest] + [least] * (amount - 1), total - largest - least * (amount - 1)
    while spare > 0:
        movable = [i for i in range(1, amount) if holding[i] < largest] or [i for i in range(1, amount) if holding[i] < limit]
        pool, budget = sum([portions[i] for i in movable]), spare
        for i in movable:
            extra = min(limit - holding[i], max(1, budget * portions[i] // pool), spare)
            holding[i] = holding[i] + extra
            spare = spare - extra
    return np.array(holding)


def noise(key, dims, scale, bound, kind=jnp.bfloat16):
    drawn = jax.random.normal(key, dims, jnp.float32) * scale
    return jnp.minimum(jnp.maximum(drawn, -bound), bound).astype(kind)


def setup_inputs(seed: int = 0) -> dict:
    splits = jax.random.split(jax.random.key(seed), 8)
    observed = draw_observed(jax.random.fold_in(splits[7], 71), 0)
    basis = noise(splits[1], (SAMPLES, NCOEF), NCOEF ** -0.5, 0.875, jnp.float32)
    taps = jnp.clip(jax.random.uniform(splits[2], (TAPS,), jnp.float32, 0.05, 0.35), 0.05, 0.35)
    epoch_owner_keys = jax.random.split(jax.random.fold_in(splits[3], 1), EPOCHS // EPD)
    epoch_owner_turns = jax.random.permutation(jax.random.fold_in(splits[3], 3), EPOCHS // EPD)
    epoch_owner = jax.vmap(lambda own, number: assign_block(jax.random.fold_in(splits[3], 2), own, number, EPD, N_SRC, 1, CAP, 2))(epoch_owner_keys, epoch_owner_turns).reshape((EPOCHS, 1))
    epoch_source = set_ends(jax.random.randint(splits[4], (EPOCHS,), 0, SRC_DEV), jax.random.fold_in(splits[4], 1), 0, SRC_DEV - 1).astype(jnp.int32)
    epoch_config = set_ends(jax.random.randint(splits[5], (EPOCHS,), 0, CONFIGS), jax.random.fold_in(splits[5], 1), 0, CONFIGS - 1).astype(jnp.int32)
    epoch_counts = draw_epoch_counts(jax.random.fold_in(splits[7], 71), 0)
    return dict(observed=observed, basis=basis, taps=taps, epoch_owner=epoch_owner, epoch_source=epoch_source, epoch_config=epoch_config, epoch_counts=epoch_counts)


exact_mode = lax.Precision.HIGHEST

def line_matrix(taps, samples):
    width = taps.shape[0]
    half = width // 2
    rows = lax.broadcasted_iota(jnp.int32, (samples, samples), 0)
    cols = lax.broadcasted_iota(jnp.int32, (samples, samples), 1)
    offset = cols - rows + half
    inside = (offset >= 0) & (offset < width)
    picked = jnp.take(taps, jnp.clip(offset, 0, width - 1))
    return jnp.where(inside, picked, jnp.zeros_like(picked))

def reference(observed, basis, taps, epoch_owner, epoch_source, epoch_config, epoch_counts):
    response = jnp.dot(line_matrix(taps, SAMPLES), basis, precision=exact_mode)
    source_of = (epoch_owner[:, 0] * SRC_DEV + epoch_source).astype(jnp.int32)
    slots = jnp.arange(EPOCHS, dtype=jnp.int32)
    live = (slots % EPD < jnp.repeat(epoch_counts, EPD)).astype(observed.dtype)
    cweight = 0.4 * (1.0 + 3.0 * jnp.arange(CONFIGS, dtype=jnp.int32).astype(observed.dtype) / CONFIGS)

    def forward(coeffs, table):
        model = jnp.dot(response, jnp.take(coeffs, source_of, axis=1), precision=exact_mode)
        model = model + jnp.take(table * cweight[None, :], epoch_config, axis=1)
        return model * live[None, :]

    def adjoint(resid):
        masked = resid * live[None, :]
        terms = jnp.dot(response.T, masked, precision=exact_mode)
        coeffs = jnp.zeros((NCOEF, SOURCES), resid.dtype).at[:, source_of].add(terms)
        table = jnp.zeros((SAMPLES, CONFIGS), resid.dtype).at[:, epoch_config].add(masked)
        return (coeffs, table * cweight[None, :])

    def param_norm(coeffs, table):
        return jnp.sqrt(jnp.sum(coeffs * coeffs) + jnp.sum(table * table))
    resid = observed * live[None, :]
    beta = jnp.sqrt(jnp.sum(resid * resid))
    resid = resid / beta
    dir_c, dir_h = adjoint(resid)
    alpha = param_norm(dir_c, dir_h)
    dir_c = dir_c / alpha
    dir_h = dir_h / alpha
    walk_c, walk_h = (dir_c, dir_h)
    sol_c = jnp.zeros_like(dir_c)
    sol_h = jnp.zeros_like(dir_h)
    phibar = beta
    rhobar = alpha
    for step in range(ITERS):
        resid = forward(dir_c, dir_h) - alpha * resid
        beta = jnp.sqrt(jnp.sum(resid * resid))
        resid = resid / beta
        back_c, back_h = adjoint(resid)
        dir_c = back_c - beta * dir_c
        dir_h = back_h - beta * dir_h
        alpha = param_norm(dir_c, dir_h)
        dir_c = dir_c / alpha
        dir_h = dir_h / alpha
        rho = jnp.sqrt(rhobar * rhobar + beta * beta)
        cosine = rhobar / rho
        sine = beta / rho
        theta = sine * alpha
        rhobar = -cosine * alpha
        phi = cosine * phibar
        phibar = sine * phibar
        sol_c = sol_c + phi / rho * walk_c
        sol_h = sol_h + phi / rho * walk_h
        walk_c = dir_c - theta / rho * walk_c
        walk_h = dir_h - theta / rho * walk_h
    return (sol_c, sol_h, walk_c, walk_h)
```

```python
import functools

import jax
import jax.numpy as jnp
from jax import lax
from jax.experimental import pallas as pl
from jax.experimental.pallas import tpu as pltpu
from jax.sharding import PartitionSpec as P

SRC_DEV = 4096
KDEV = 16
F = 64
MESH = pl.DeviceIdType.MESH
HIGHEST = lax.Precision.HIGHEST
f32, bf16 = jnp.float32, jnp.bfloat16


def iota(shape, dim):
    return lax.broadcasted_iota(jnp.int32, shape, dim)


def pieces(x, count):
    out = []
    for _ in range(count - 1):
        head = x.astype(bf16)
        out.append(head)
        x = x - head.astype(f32)
    out.append(x.astype(bf16))
    return out


def dot3(a, b):
    ah, al = pieces(a, 2)
    bh, bl = pieces(b, 2)
    return jnp.dot(
        jnp.concatenate([ah, al, ah], 1),
        jnp.concatenate([bh, bh, bl], 0),
        preferred_element_type=f32,
    )


def exact(a, b, dims=(((1,), (0,)), ((), ()))):
    return lax.dot_general(a, b, dims, precision=HIGHEST, preferred_element_type=f32)


def fold(onehot, x):
    width = x.shape[1]
    got = lax.dot_general(
        onehot, jnp.concatenate(pieces(x, 3), 1), (((0,), (0,)), ((), ())), preferred_element_type=f32
    )
    return got[:, :width] + got[:, width : 2 * width] + got[:, 2 * width :]


def total(x):
    return jnp.sum(x, axis=(0, 1), keepdims=True)


def scalar_rows(*values):
    lane, row = iota((8, 2 * F), 1), iota((8, 2 * F), 0)
    out = jnp.zeros((8, 2 * F), f32)
    for at, value in enumerate(values):
        out = jnp.where((lane == at) & (row == 0), value, out)
    return out


def lanczos(
    dims,
    obs, basis, taps, owner, source, config, counts,
    z_out, xh_out, wh_out,
    send, recv, slots, quads, c0s, cgs, nss, v2s, v3s, rpad,
    a1, a2, b1, b2, d1, d2,
    send_sem, recv_sem, fsend_sem, frecv_sem, xsend, xrecv, ysend, yrecv,
):
    n_src, n_inst, rows, configs, hi_n, lo_n, chunk = dims
    me, mine = lax.axis_index("src"), lax.axis_index("inst")
    my_hi, my_lo = me // lo_n, lax.rem(me, lo_n)
    samples, epochs = obs.shape
    coefs = basis.shape[1]
    half_rows = n_inst * n_src * rows
    steps = 2 * half_rows // chunk

    barrier = pltpu.get_barrier_semaphore()
    for step in range(1, n_src):
        pl.semaphore_signal(barrier, inc=1, device_id=(lax.rem(me + step, n_src), mine), device_id_type=MESH)
    for step in range(1, n_inst):
        pl.semaphore_signal(barrier, inc=1, device_id=(me, lax.rem(mine + step, n_inst)), device_id_type=MESH)

    own = owner[...]
    table = own == iota((n_src, epochs), 0)
    before = (iota((epochs, epochs), 0) < iota((epochs, epochs), 1)).astype(bf16)
    counted = jnp.dot(table.astype(bf16), before, preferred_element_type=f32)
    slot = jnp.sum(jnp.where(table, counted, 0.0), axis=0, keepdims=True).astype(jnp.int32)
    live = iota((1, epochs), 1) < counts[...]
    upper = slot >= rows
    place = jnp.where(live, own * rows + slot - jnp.where(upper, rows, 0), -1)
    hit = place == iota((n_src * rows, epochs), 0)
    data = jnp.concatenate(
        [
            obs[...],
            (source[...] + 1).astype(f32),
            config[...].astype(f32),
            jnp.ones((1, epochs), f32),
            jnp.zeros((F - samples - 3, epochs), f32),
        ],
        0,
    )
    stacked = jnp.concatenate(pieces(data, 3), 0)

    def packed(mask):
        got = lax.dot_general(
            mask.astype(bf16), stacked, (((1,), (1,)), ((), ())), preferred_element_type=f32
        )
        return got[:, :F] + got[:, F : 2 * F] + got[:, 2 * F :]

    send[...] = jnp.concatenate([packed(hit & ~upper), packed(hit & upper)], 1).reshape(n_src, rows, 2 * F)
    recv[mine, me] = send[me]

    pl.semaphore_wait(barrier, n_src + n_inst - 2)
    for step in range(1, n_src):
        peer = lax.rem(me + step, n_src)
        pltpu.make_async_remote_copy(
            send.at[peer], recv.at[mine, me], send_sem.at[peer], recv_sem.at[me],
            device_id=(peer, mine), device_id_type=MESH,
        ).start()

    spread = jnp.zeros((samples, samples), f32)
    offset = iota((samples, samples), 1) - iota((samples, samples), 0) + taps.shape[0] // 2
    for tap in range(taps.shape[0]):
        spread = jnp.where(offset == tap, taps[tap], spread)
    rpad[...] = jnp.zeros((F, F), f32)
    rpad[pl.ds(0, samples), pl.ds(0, coefs)] = exact(spread, basis[...])
    resp = rpad[...]
    gram = exact(resp, resp, (((0,), (0,)), ((), ())))
    cweight = 0.4 * (1.0 + 3.0 * iota((configs, 1), 0).astype(f32) / configs)

    for step in range(1, n_src):
        peer = lax.rem(me + step, n_src)
        pltpu.make_async_remote_copy(
            send.at[peer], recv.at[mine, peer], send_sem.at[peer], recv_sem.at[peer],
            device_id=(peer, mine), device_id_type=MESH,
        ).wait()
    forwards = []
    for step in range(1, n_inst):
        other = lax.rem(mine + step, n_inst)
        pltpu.make_async_remote_copy(
            recv.at[mine], recv.at[mine], fsend_sem.at[other], frecv_sem.at[mine],
            device_id=(me, other), device_id_type=MESH,
        ).start()
        forwards.append(
            pltpu.make_async_remote_copy(
                recv.at[mine], recv.at[other], fsend_sem.at[other], frecv_sem.at[other],
                device_id=(me, other), device_id_type=MESH,
            )
        )
    for forward in forwards:
        forward.wait()

    held = recv[...].reshape(half_rows, 2 * F)
    slots[pl.ds(0, half_rows), :] = held[:, :F]
    slots[pl.ds(half_rows, half_rows), :] = held[:, F:]
    pick = (iota((8, 2 * F), 1) == samples + F * iota((8, 2 * F), 0)).astype(f32)
    names = exact(pick, held, (((1,), (1,)), ((), ())))
    id_row = jnp.concatenate([names[0:1], names[1:2]], 1)
    lane = iota((1, F), 1)

    def at(step):
        return pl.ds(pl.multiple_of(step * chunk, chunk), chunk)

    def config_table(part):
        return (
            (part[:, samples + 1 : samples + 2] == iota((chunk, configs), 1).astype(f32))
            & (part[:, samples + 2 : samples + 3] > 0.5)
        ).astype(bf16)

    def project(step, carry):
        part = slots[at(step), :]
        spectra = jnp.where(lane < samples, part, 0.0)
        quads[at(step), :] = jnp.concatenate(
            pieces(dot3(spectra, resp), 3) + [config_table(part)], 1
        )
        return carry + total(spectra * spectra)

    one = jnp.zeros((1, 1), f32)
    b_sq = lax.fori_loop(0, steps, project, one)

    def gather(step, carry):
        stats, c_sq, quad = carry
        part = slots[at(step), :]
        name = part[:, samples : samples + 1]
        same = ((name == id_row) & (name > 0.5)).astype(bf16)
        got = jnp.dot(same, quads[...], preferred_element_type=f32)
        c0 = got[:, :F] + got[:, F : 2 * F] + got[:, 2 * F : 3 * F]
        named = got[:, 3 * F :]
        count = jnp.sum(named, axis=1, keepdims=True)
        cg = dot3(c0, gram)
        c0s[at(step), :] = c0
        cgs[at(step), :] = cg
        nss[at(step), :] = named
        stats = stats + fold(config_table(part), jnp.concatenate([part, c0], 1))
        return stats, c_sq + total(c0 * c0 / jnp.maximum(count, 1.0)), quad + total(c0 * cg)

    stats, c_sq, quad = lax.fori_loop(0, steps, gather, (jnp.zeros((configs, 2 * F), f32), one, one))

    def swap(which, value, one_buf, two_buf):
        one_buf[my_hi] = value
        sent = []
        for step in range(1, hi_n):
            peer = lax.rem(my_hi + step, hi_n)
            pltpu.make_async_remote_copy(
                one_buf.at[my_hi], one_buf.at[my_hi], xsend.at[which, peer], xrecv.at[which, my_hi],
                device_id=(peer * lo_n + my_lo, mine), device_id_type=MESH,
            ).start()
            sent.append(pltpu.make_async_remote_copy(
                one_buf.at[my_hi], one_buf.at[peer], xsend.at[which, peer], xrecv.at[which, peer],
                device_id=(peer * lo_n + my_lo, mine), device_id_type=MESH,
            ))
        for copy in sent:
            copy.wait()
        two_buf[my_lo] = jnp.sum(one_buf[...], axis=0)
        sent = []
        for step in range(1, lo_n):
            peer = lax.rem(my_lo + step, lo_n)
            pltpu.make_async_remote_copy(
                two_buf.at[my_lo], two_buf.at[my_lo], ysend.at[which, peer], yrecv.at[which, my_lo],
                device_id=(my_hi * lo_n + peer, mine), device_id_type=MESH,
            ).start()
            sent.append(pltpu.make_async_remote_copy(
                two_buf.at[my_lo], two_buf.at[peer], ysend.at[which, peer], yrecv.at[which, peer],
                device_id=(my_hi * lo_n + peer, mine), device_id_type=MESH,
            ))
        for copy in sent:
            copy.wait()
        return jnp.sum(two_buf[...], axis=0)

    got = swap(0, jnp.concatenate([stats, scalar_rows(b_sq, c_sq, quad)], 0), a1, a2)
    b_sq, c_sq, quad = [got[configs : configs + 1, i : i + 1] for i in range(3)]
    per_config = got[:configs, samples + 2 : samples + 3]
    h0 = jnp.where(lane < samples, got[:configs, :F], 0.0) * cweight
    p_sq = c_sq + total(h0 * h0)
    inv_p = 1.0 / jnp.sqrt(p_sq)
    beta1 = jnp.sqrt(b_sq)
    alpha1 = jnp.sqrt(p_sq) / beta1

    def table_step(h, s):
        hr = exact(cweight * h, resp)
        mh = cweight * (exact(s, resp, (((1,), (1,)), ((), ()))) + per_config * cweight * h)
        return hr, mh, total(hr * s) + total(h * mh)

    h1 = h0 * inv_p
    hr1, mh1, extra = table_step(h1, got[:configs, F:] * inv_p)
    diag1 = quad * inv_p * inv_p + extra
    beta2 = jnp.sqrt(diag1 - alpha1 * alpha1)

    def second(step, carry):
        stats, v_sq, quad = carry
        named = nss[at(step), :]
        count = jnp.sum(named, axis=1, keepdims=True)
        v2 = (count * cgs[at(step), :] - diag1 * c0s[at(step), :]) * inv_p + dot3(named, hr1)
        vg = dot3(v2, gram)
        v2s[at(step), :] = v2
        cgs[at(step), :] = vg
        stats = stats + fold(config_table(slots[at(step), :]), v2)
        return stats, v_sq + total(v2 * v2 / jnp.maximum(count, 1.0)), quad + total(v2 * vg)

    stats, v_sq, quad = lax.fori_loop(0, steps, second, (jnp.zeros((configs, F), f32), one, one))
    wide = jnp.concatenate([stats[: configs // 2], stats[configs // 2 :]], 1)
    got = swap(1, jnp.concatenate([wide, scalar_rows(v_sq, quad)], 0), b1, b2)
    v_sq, quad = [got[configs // 2 : configs // 2 + 1, i : i + 1] for i in range(2)]
    h2 = mh1 - diag1 * h1
    off_sq = v_sq + total(h2 * h2)
    off1 = jnp.sqrt(off_sq)
    inv1 = 1.0 / off1
    h2 = h2 * inv1
    s2 = jnp.concatenate([got[: configs // 2, :F], got[: configs // 2, F:]], 0) * inv1
    hr2, mh2, extra = table_step(h2, s2)
    diag2 = quad * inv1 * inv1 + extra
    alpha2 = off1 / beta2
    beta3 = jnp.sqrt(diag2 - alpha2 * alpha2)

    def third(step, v_sq):
        named = nss[at(step), :]
        count = jnp.sum(named, axis=1, keepdims=True)
        v3 = (
            (count * cgs[at(step), :] - diag2 * v2s[at(step), :]) * inv1
            - (off1 * inv_p) * c0s[at(step), :]
            + dot3(named, hr2)
        )
        v3s[at(step), :] = v3
        return v_sq + total(v3 * v3 / jnp.maximum(count, 1.0))

    v_sq = lax.fori_loop(0, steps, third, one)
    got = swap(2, scalar_rows(v_sq), d1, d2)
    h3 = mh2 - diag2 * h2 - off1 * h1
    off2 = jnp.sqrt(got[0:1, 0:1] + total(h3 * h3))
    inv2 = 1.0 / off2
    alpha3 = off2 / beta3

    rho1 = jnp.sqrt(alpha1 * alpha1 + beta2 * beta2)
    cos1, sin1 = alpha1 / rho1, beta2 / rho1
    turn1, rhobar = sin1 * alpha2 / rho1, -cos1 * alpha2
    move1, phibar = cos1 * beta1 / rho1, sin1 * beta1
    rho2 = jnp.sqrt(rhobar * rhobar + beta3 * beta3)
    cos2, sin2 = rhobar / rho2, beta3 / rho2
    turn2, move2 = sin2 * alpha3 / rho2, cos2 * phibar / rho2

    walk = h2 - turn1 * h1
    xh_out[...] = move1 * h1 + move2 * walk
    wh_out[...] = inv2 * h3 - turn2 * walk

    def finish(step, carry):
        count = jnp.sum(nss[at(step), :], axis=1, keepdims=True)
        share = 1.0 / jnp.maximum(count, 1.0)
        v1 = c0s[at(step), :] * inv_p
        walk = v2s[at(step), :] * inv1 - turn1 * v1
        x = (move1 * v1 + move2 * walk) * share
        w = (inv2 * v3s[at(step), :] - turn2 * walk) * share
        x = jnp.where(lane == samples, slots[at(step), :], x)
        z_out[at(step), :] = jnp.concatenate([x, w], 1)
        return carry

    lax.fori_loop(0, steps, finish, 0)


def spread_out(samples, coefs, z_ref, x_ref, w_ref, zt, name):
    block = x_ref.shape[1]

    @pl.when(pl.program_id(0) == 0)
    def _():
        z = z_ref[...]
        flat = z.T
        head = flat.astype(bf16)
        zt[pl.ds(0, 2 * F), :] = head
        zt[pl.ds(2 * F, 2 * F), :] = (flat - head.astype(f32)).astype(bf16)
        name[...] = z[:, samples : samples + 1].astype(jnp.int32) - 1

    first = pl.program_id(0) * block
    hit = (name[...] == iota((z_ref.shape[0], block), 1) + first).astype(bf16)
    got = jnp.dot(zt[...], hit, preferred_element_type=f32)
    got = got[: 2 * F] + got[2 * F :]
    x_ref[...] = got[:coefs]
    w_ref[...] = got[F : F + coefs]


def on_device(observed, basis, taps, epoch_owner, epoch_source, epoch_config, epoch_counts):
    n_src, n_inst = lax.axis_size("src"), lax.axis_size("inst")
    samples, epochs = observed.shape
    coefs = basis.shape[1]
    cap = max(2, epochs * 3 // (2 * n_src))
    rows = -(-cap // 16) * 8
    configs = KDEV * n_inst
    lo_n = 1
    while lo_n * lo_n * 4 <= n_src:
        lo_n *= 2
    hi_n = n_src // lo_n
    slots = 2 * rows * n_src * n_inst
    chunk = 512
    dims = (n_src, n_inst, rows, configs, hi_n, lo_n, chunk)
    vmem, smem = pl.BlockSpec(memory_space=pltpu.VMEM), pl.BlockSpec(memory_space=pltpu.SMEM)
    z, xh, wh = pl.pallas_call(
        functools.partial(lanczos, dims),
        out_shape=(
            jax.ShapeDtypeStruct((slots, 2 * F), f32),
            jax.ShapeDtypeStruct((configs, F), f32),
            jax.ShapeDtypeStruct((configs, F), f32),
        ),
        in_specs=[vmem, vmem, smem, vmem, vmem, vmem, vmem],
        out_specs=(vmem, vmem, vmem),
        scratch_shapes=[
            pltpu.VMEM((n_src, rows, 2 * F), f32),
            pltpu.VMEM((n_inst, n_src, rows, 2 * F), f32),
            pltpu.VMEM((slots, F), f32),
            pltpu.VMEM((slots, 3 * F + configs), bf16),
            pltpu.VMEM((slots, F), f32),
            pltpu.VMEM((slots, F), f32),
            pltpu.VMEM((slots, configs), f32),
            pltpu.VMEM((slots, F), f32),
            pltpu.VMEM((slots, F), f32),
            pltpu.VMEM((F, F), f32),
            pltpu.VMEM((hi_n, configs + 8, 2 * F), f32),
            pltpu.VMEM((lo_n, configs + 8, 2 * F), f32),
            pltpu.VMEM((hi_n, configs // 2 + 8, 2 * F), f32),
            pltpu.VMEM((lo_n, configs // 2 + 8, 2 * F), f32),
            pltpu.VMEM((hi_n, 8, 2 * F), f32),
            pltpu.VMEM((lo_n, 8, 2 * F), f32),
            pltpu.SemaphoreType.DMA((n_src,)),
            pltpu.SemaphoreType.DMA((n_src,)),
            pltpu.SemaphoreType.DMA((n_inst,)),
            pltpu.SemaphoreType.DMA((n_inst,)),
            pltpu.SemaphoreType.DMA((3, hi_n)),
            pltpu.SemaphoreType.DMA((3, hi_n)),
            pltpu.SemaphoreType.DMA((3, lo_n)),
            pltpu.SemaphoreType.DMA((3, lo_n)),
        ],
        compiler_params=pltpu.CompilerParams(
            collective_id=0, has_side_effects=True, vmem_limit_bytes=60 * 1024 * 1024
        ),
        name="lanczos",
    )(
        observed,
        basis,
        taps,
        epoch_owner.reshape(1, epochs),
        epoch_source.reshape(1, epochs),
        epoch_config.reshape(1, epochs),
        epoch_counts.reshape(1, 1),
    )
    block = 512
    sol_c, walk_c = pl.pallas_call(
        functools.partial(spread_out, samples, coefs),
        grid=(SRC_DEV // block,),
        out_shape=(jax.ShapeDtypeStruct((coefs, SRC_DEV), f32),) * 2,
        in_specs=[pl.BlockSpec((slots, 2 * F), lambda i: (0, 0))],
        out_specs=(pl.BlockSpec((coefs, block), lambda i: (0, i)),) * 2,
        scratch_shapes=[pltpu.VMEM((4 * F, slots), bf16), pltpu.VMEM((slots, 1), jnp.int32)],
        compiler_params=pltpu.CompilerParams(vmem_limit_bytes=60 * 1024 * 1024),
        name="spread_out",
    )(z)
    start = lax.axis_index("inst") * KDEV
    sol_h = lax.dynamic_slice_in_dim(xh, start, KDEV, 0)[:, :samples].T
    walk_h = lax.dynamic_slice_in_dim(wh, start, KDEV, 0)[:, :samples].T
    return (sol_c, sol_h, walk_c, walk_h)


def solution(mesh):
    placed = (
        P(None, ("src", "inst")),
        P(),
        P(),
        P(("src", "inst"), None),
        P(("src", "inst")),
        P(("src", "inst")),
        P(("src", "inst")),
    )
    return jax.shard_map(
        on_device,
        mesh=mesh,
        in_specs=placed,
        out_specs=(P(None, "src"), P(None, "inst"), P(None, "src"), P(None, "inst")),
        check_vma=False,
    )
```

```python
import functools

import jax
import jax.numpy as jnp
from jax import lax
from jax.experimental import pallas as pl
from jax.experimental.pallas import tpu as pltpu
from jax.sharding import PartitionSpec as P

SRC_DEV = 4096
KDEV = 16
F = 64
MESH = pl.DeviceIdType.MESH
HIGHEST = lax.Precision.HIGHEST
f32, bf16 = jnp.float32, jnp.bfloat16


def iota(shape, dim):
    return lax.broadcasted_iota(jnp.int32, shape, dim)


def pieces(x, count):
    out = []
    for _ in range(count - 1):
        head = x.astype(bf16)
        out.append(head)
        x = x - head.astype(f32)
    out.append(x.astype(bf16))
    return out


def dot3(a, b):
    ah, al = pieces(a, 2)
    bh, bl = pieces(b, 2)
    return jnp.dot(
        jnp.concatenate([ah, al, ah], 1),
        jnp.concatenate([bh, bh, bl], 0),
        preferred_element_type=f32,
    )


def exact(a, b, dims=(((1,), (0,)), ((), ()))):
    return lax.dot_general(a, b, dims, precision=HIGHEST, preferred_element_type=f32)


def fold(onehot, x):
    width = x.shape[1]
    got = lax.dot_general(
        onehot, jnp.concatenate(pieces(x, 3), 1), (((0,), (0,)), ((), ())), preferred_element_type=f32
    )
    return got[:, :width] + got[:, width : 2 * width] + got[:, 2 * width :]


def total(x):
    return jnp.sum(x, axis=(0, 1), keepdims=True)


def stack8(x):
    return jnp.sum(x.reshape(x.shape[0] // 8, 8, x.shape[1]), axis=0)


def with_scalars(block, first, *values):
    lane, row = iota(block.shape, 1), iota(block.shape, 0)
    for at, value in enumerate(values):
        block = jnp.where((lane == first + at) & (row == 0), value, block)
    return block


def lanczos(
    dims,
    obs, basis_t, taps, owner, source, config, counts,
    z_out, xh_out, wh_out,
    send, recv, slots, quads, c0s, cgs, nss, counted, share, v2s, v3s, rpad, tables,
    a1, a2, b1, b2, norms,
    send_sem, recv_sem, fsend_sem, frecv_sem, xsend, xrecv, ysend, yrecv, nsend, nrecv,
):
    n_src, n_inst, rows, configs, hi_n, lo_n, chunk = dims
    me, mine = lax.axis_index("src"), lax.axis_index("inst")
    my_hi, my_lo = me // lo_n, lax.rem(me, lo_n)
    samples, epochs = obs.shape
    coefs = basis_t.shape[0]
    half_rows = n_inst * n_src * rows
    steps = 2 * half_rows // chunk

    barrier = pltpu.get_barrier_semaphore()
    for step in range(1, n_src):
        pl.semaphore_signal(barrier, inc=1, device_id=(lax.rem(me + step, n_src), mine), device_id_type=MESH)
    for step in range(1, n_inst):
        pl.semaphore_signal(barrier, inc=1, device_id=(me, lax.rem(mine + step, n_inst)), device_id_type=MESH)

    own = owner[...]
    table = own == iota((n_src, epochs), 0)
    before = (iota((epochs, epochs), 0) < iota((epochs, epochs), 1)).astype(bf16)
    earlier = jnp.dot(table.astype(bf16), before, preferred_element_type=f32)
    slot = jnp.sum(jnp.where(table, earlier, 0.0), axis=0, keepdims=True).astype(jnp.int32)
    live = iota((1, epochs), 1) < counts[...]
    upper = slot >= rows
    place = jnp.where(live, own * rows + slot - jnp.where(upper, rows, 0), -1)
    hit = place == iota((n_src * rows, epochs), 0)
    data = jnp.concatenate(
        [
            obs[...],
            (source[...] + 1).astype(f32),
            config[...].astype(f32),
            jnp.ones((1, epochs), f32),
            jnp.zeros((F - samples - 3, epochs), f32),
        ],
        0,
    )
    stacked = jnp.concatenate(pieces(data, 3), 0)

    def packed(mask):
        got = lax.dot_general(
            mask.astype(bf16), stacked, (((1,), (1,)), ((), ())), preferred_element_type=f32
        )
        return got[:, :F] + got[:, F : 2 * F] + got[:, 2 * F :]

    send[...] = jnp.concatenate([packed(hit & ~upper), packed(hit & upper)], 1).reshape(n_src, rows, 2 * F)
    recv[mine, me] = send[me]

    pl.semaphore_wait(barrier, n_src + n_inst - 2)
    for step in range(1, n_src):
        peer = lax.rem(me + step, n_src)
        pltpu.make_async_remote_copy(
            send.at[peer], recv.at[mine, me], send_sem.at[peer], recv_sem.at[me],
            device_id=(peer, mine), device_id_type=MESH,
        ).start()

    spread = jnp.zeros((samples, samples), f32)
    offset = iota((samples, samples), 1) - iota((samples, samples), 0) + taps.shape[0] // 2
    for tap in range(taps.shape[0]):
        spread = jnp.where(offset == tap, taps[tap], spread)
    rpad[...] = jnp.zeros((F, F), f32)
    rpad[pl.ds(0, samples), pl.ds(0, coefs)] = exact(spread, basis_t[...], (((1,), (1,)), ((), ())))
    resp = rpad[...]
    gram = exact(resp, resp, (((0,), (0,)), ((), ())))
    resp_t = resp.T
    cweight = 0.4 * (1.0 + 3.0 * iota((configs, 1), 0).astype(f32) / configs)

    for step in range(1, n_src):
        peer = lax.rem(me + step, n_src)
        pltpu.make_async_remote_copy(
            send.at[peer], recv.at[mine, peer], send_sem.at[peer], recv_sem.at[peer],
            device_id=(peer, mine), device_id_type=MESH,
        ).wait()
    forwards = []
    for step in range(1, n_inst):
        other = lax.rem(mine + step, n_inst)
        pltpu.make_async_remote_copy(
            recv.at[mine], recv.at[mine], fsend_sem.at[other], frecv_sem.at[mine],
            device_id=(me, other), device_id_type=MESH,
        ).start()
        forwards.append(
            pltpu.make_async_remote_copy(
                recv.at[mine], recv.at[other], fsend_sem.at[other], frecv_sem.at[other],
                device_id=(me, other), device_id_type=MESH,
            )
        )
    for forward in forwards:
        forward.wait()

    held = recv[...].reshape(half_rows, 2 * F)
    slots[pl.ds(0, half_rows), :] = held[:, :F]
    slots[pl.ds(half_rows, half_rows), :] = held[:, F:]
    pick = (iota((8, 2 * F), 1) == samples + F * iota((8, 2 * F), 0)).astype(bf16)
    names = sum(
        lax.dot_general(pick, piece, (((1,), (1,)), ((), ())), preferred_element_type=f32)
        for piece in pieces(held, 2)
    )
    id_row = jnp.concatenate([names[0:1], names[1:2]], 1)
    lane = iota((1, F), 1)

    def at(step):
        return pl.ds(pl.multiple_of(step * chunk, chunk), chunk)

    def config_table(part):
        return (
            (part[:, samples + 1 : samples + 2] == iota((chunk, configs), 1).astype(f32))
            & (part[:, samples + 2 : samples + 3] > 0.5)
        ).astype(bf16)

    def project(step, carry):
        part = slots[at(step), :]
        spectra = jnp.where(lane < samples, part, 0.0)
        quads[at(step), :] = jnp.concatenate(
            pieces(dot3(spectra, resp), 2)
            + [jnp.broadcast_to(part[:, samples + 2 : samples + 3], (chunk, F)).astype(bf16), config_table(part)],
            1,
        )
        return carry + stack8(spectra * spectra)

    none = jnp.zeros((8, F), f32)
    unroll = steps <= 4
    b_sq = total(lax.fori_loop(0, steps, project, none, unroll=unroll))

    def gather(step, carry):
        stats, c_sq, quad = carry
        part = slots[at(step), :]
        name = part[:, samples : samples + 1]
        same = ((name == id_row) & (name > 0.5)).astype(bf16)
        got = jnp.dot(same, quads[...], preferred_element_type=f32)
        c0 = got[:, :F] + got[:, F : 2 * F]
        count = got[:, 2 * F : 3 * F]
        weight = 1.0 / jnp.maximum(count, 1.0)
        cg = dot3(c0, gram)
        c0s[at(step), :] = c0
        cgs[at(step), :] = count * cg
        nss[at(step), :] = got[:, 3 * F :]
        counted[at(step), :] = count
        share[at(step), :] = weight
        stats = stats + fold(config_table(part), jnp.concatenate([part, c0], 1))
        return stats, c_sq + stack8(c0 * c0 * weight), quad + stack8(c0 * cg)

    stats, c_sq, quad = lax.fori_loop(
        0, steps, gather, (jnp.zeros((configs, 2 * F), f32), none, none), unroll=unroll
    )

    def swap(which, value, one_buf, two_buf):
        one_buf[my_hi] = value
        sent = []
        for step in range(1, hi_n):
            peer = lax.rem(my_hi + step, hi_n)
            pltpu.make_async_remote_copy(
                one_buf.at[my_hi], one_buf.at[my_hi], xsend.at[which, peer], xrecv.at[which, my_hi],
                device_id=(peer * lo_n + my_lo, mine), device_id_type=MESH,
            ).start()
            sent.append(pltpu.make_async_remote_copy(
                one_buf.at[my_hi], one_buf.at[peer], xsend.at[which, peer], xrecv.at[which, peer],
                device_id=(peer * lo_n + my_lo, mine), device_id_type=MESH,
            ))
        for copy in sent:
            copy.wait()
        two_buf[my_lo] = jnp.sum(one_buf[...], axis=0)
        sent = []
        for step in range(1, lo_n):
            peer = lax.rem(my_lo + step, lo_n)
            pltpu.make_async_remote_copy(
                two_buf.at[my_lo], two_buf.at[my_lo], ysend.at[which, peer], yrecv.at[which, my_lo],
                device_id=(my_hi * lo_n + peer, mine), device_id_type=MESH,
            ).start()
            sent.append(pltpu.make_async_remote_copy(
                two_buf.at[my_lo], two_buf.at[peer], ysend.at[which, peer], yrecv.at[which, peer],
                device_id=(my_hi * lo_n + peer, mine), device_id_type=MESH,
            ))
        for copy in sent:
            copy.wait()
        return jnp.sum(two_buf[...], axis=0)

    spare = 2 * F - 4
    got = swap(0, with_scalars(stats, spare, b_sq, total(c_sq), total(quad)), a1, a2)
    b_sq, c_sq, quad = [got[0:1, spare + i : spare + i + 1] for i in range(3)]
    per_config = got[:configs, samples + 2 : samples + 3]
    h0 = jnp.where(lane < samples, got[:configs, :F], 0.0) * cweight
    p_sq = c_sq + total(h0 * h0)
    inv_p = 1.0 / jnp.sqrt(p_sq)
    beta1 = jnp.sqrt(b_sq)
    alpha1 = jnp.sqrt(p_sq) / beta1

    def table_step(h, s):
        hr = dot3(cweight * h, resp)
        mh = cweight * (dot3(s, resp_t) + per_config * cweight * h)
        return hr, mh, total(hr * s) + total(h * mh)

    h1 = h0 * inv_p
    hr1, mh1, extra = table_step(h1, jnp.where(lane < coefs, got[:, F:], 0.0) * inv_p)
    diag1 = quad * inv_p * inv_p + extra
    beta2 = jnp.sqrt(diag1 - alpha1 * alpha1)

    def second(step, carry):
        stats, v_sq, quad = carry
        v2 = (cgs[at(step), :] - diag1 * c0s[at(step), :]) * inv_p + dot3(nss[at(step), :], hr1)
        vg = dot3(v2, gram)
        v2s[at(step), :] = v2
        cgs[at(step), :] = counted[at(step), :] * vg
        stats = stats + fold(quads[at(step), 3 * F :], v2)
        return stats, v_sq + stack8(v2 * v2 * share[at(step), :]), quad + stack8(v2 * vg)

    stats, v_sq, quad = lax.fori_loop(
        0, steps, second, (jnp.zeros((configs, F), f32), none, none), unroll=unroll
    )
    wide = jnp.concatenate([stats[: configs // 2], stats[configs // 2 :]], 1)
    got = swap(1, with_scalars(wide, spare, total(v_sq), total(quad)), b1, b2)
    v_sq, quad = [got[0:1, spare + i : spare + i + 1] for i in range(2)]
    h2 = mh1 - diag1 * h1
    off_sq = v_sq + total(h2 * h2)
    off1 = jnp.sqrt(off_sq)
    inv1 = 1.0 / off1
    h2 = h2 * inv1
    s2 = jnp.where(lane < coefs, jnp.concatenate([got[:, :F], got[:, F:]], 0), 0.0) * inv1
    hr2, mh2, extra = table_step(h2, s2)
    diag2 = quad * inv1 * inv1 + extra
    alpha2 = off1 / beta2
    beta3 = jnp.sqrt(diag2 - alpha2 * alpha2)

    def third(step, v_sq):
        v3 = (
            (cgs[at(step), :] - diag2 * v2s[at(step), :]) * inv1
            - (off1 * inv_p) * c0s[at(step), :]
            + dot3(nss[at(step), :], hr2)
        )
        v3s[at(step), :] = v3
        return v_sq + stack8(v3 * v3 * share[at(step), :])

    v_sq = lax.fori_loop(0, steps, third, none, unroll=unroll)
    norms[me] = jnp.concatenate([v_sq, none], 1)
    sent = []
    for step in range(1, n_src):
        peer = lax.rem(me + step, n_src)
        pltpu.make_async_remote_copy(
            norms.at[me], norms.at[me], nsend.at[peer], nrecv.at[me],
            device_id=(peer, mine), device_id_type=MESH,
        ).start()
        sent.append(pltpu.make_async_remote_copy(
            norms.at[me], norms.at[peer], nsend.at[peer], nrecv.at[peer],
            device_id=(peer, mine), device_id_type=MESH,
        ))
    for copy in sent:
        copy.wait()
    v_sq = total(jnp.sum(norms[...], axis=0))
    h3 = mh2 - diag2 * h2 - off1 * h1
    off2 = jnp.sqrt(v_sq + total(h3 * h3))
    inv2 = 1.0 / off2
    alpha3 = off2 / beta3

    rho1 = jnp.sqrt(alpha1 * alpha1 + beta2 * beta2)
    cos1, sin1 = alpha1 / rho1, beta2 / rho1
    turn1, rhobar = sin1 * alpha2 / rho1, -cos1 * alpha2
    move1, phibar = cos1 * beta1 / rho1, sin1 * beta1
    rho2 = jnp.sqrt(rhobar * rhobar + beta3 * beta3)
    cos2, sin2 = rhobar / rho2, beta3 / rho2
    turn2, move2 = sin2 * alpha3 / rho2, cos2 * phibar / rho2

    walk = h2 - turn1 * h1
    tables[0] = move1 * h1 + move2 * walk
    tables[1] = inv2 * h3 - turn2 * walk
    kept = configs // n_inst
    xh_out[...] = tables[0, pl.ds(pl.multiple_of(mine * kept, kept), kept), pl.ds(0, samples)]
    wh_out[...] = tables[1, pl.ds(pl.multiple_of(mine * kept, kept), kept), pl.ds(0, samples)]

    def finish(step, carry):
        v1 = c0s[at(step), :] * inv_p
        walk = v2s[at(step), :] * inv1 - turn1 * v1
        x = (move1 * v1 + move2 * walk) * share[at(step), :]
        w = (inv2 * v3s[at(step), :] - turn2 * walk) * share[at(step), :]
        x = jnp.where(lane == samples, slots[at(step), :], x)
        z_out[at(step), :] = jnp.concatenate([x, w], 1)
        return carry

    lax.fori_loop(0, steps, finish, 0, unroll=unroll)


def spread_out(samples, coefs, z_ref, xh_ref, wh_ref, x_ref, w_ref, xt_ref, wt_ref, zt, match):
    lanes = match.shape[1]

    @pl.when(pl.program_id(0) == 0)
    def _():
        z = z_ref[...]
        flat = z.T
        head = flat.astype(bf16)
        zt[pl.ds(0, 2 * F), :] = head
        zt[pl.ds(2 * F, 2 * F), :] = (flat - head.astype(f32)).astype(bf16)
        name = z[:, samples : samples + 1].astype(jnp.int32) - 1
        match[...] = jnp.where((name & (lanes - 1)) == iota(match.shape, 1), name // lanes, -1).astype(f32).astype(bf16)
        xt_ref[...] = xh_ref[...]
        wt_ref[...] = wh_ref[...]

    groups = x_ref.shape[1] // lanes
    first = pl.program_id(0) * groups
    hit = jnp.concatenate(
        [
            jnp.where(match[...] == (first + i).astype(f32).astype(bf16), 1.0, 0.0).astype(bf16)
            for i in range(groups)
        ],
        1,
    )
    got = jnp.dot(zt[...], hit, preferred_element_type=f32)
    got = got[: 2 * F] + got[2 * F :]
    x_ref[...] = got[:coefs]
    w_ref[...] = got[F : F + coefs]


def on_device(observed, basis, taps, epoch_owner, epoch_source, epoch_config, epoch_counts):
    n_src, n_inst = lax.axis_size("src"), lax.axis_size("inst")
    samples, epochs = observed.shape
    coefs = basis.shape[1]
    cap = max(2, epochs * 3 // (2 * n_src))
    rows = -(-cap // 16) * 8
    configs = KDEV * n_inst
    lo_n = 1
    while lo_n * lo_n * 4 <= n_src:
        lo_n *= 2
    hi_n = n_src // lo_n
    slots = 2 * rows * n_src * n_inst
    chunk = 512
    dims = (n_src, n_inst, rows, configs, hi_n, lo_n, chunk)
    vmem, smem = pl.BlockSpec(memory_space=pltpu.VMEM), pl.BlockSpec(memory_space=pltpu.SMEM)
    z, xh, wh = pl.pallas_call(
        functools.partial(lanczos, dims),
        out_shape=(
            jax.ShapeDtypeStruct((slots, 2 * F), f32),
            jax.ShapeDtypeStruct((KDEV, samples), f32),
            jax.ShapeDtypeStruct((KDEV, samples), f32),
        ),
        in_specs=[vmem, vmem, smem, vmem, vmem, vmem, vmem],
        out_specs=(vmem, vmem, vmem),
        scratch_shapes=[
            pltpu.VMEM((n_src, rows, 2 * F), f32),
            pltpu.VMEM((n_inst, n_src, rows, 2 * F), f32),
            pltpu.VMEM((slots, F), f32),
            pltpu.VMEM((slots, 3 * F + configs), bf16),
            pltpu.VMEM((slots, F), f32),
            pltpu.VMEM((slots, F), f32),
            pltpu.VMEM((slots, configs), f32),
            pltpu.VMEM((slots, F), f32),
            pltpu.VMEM((slots, F), f32),
            pltpu.VMEM((slots, F), f32),
            pltpu.VMEM((slots, F), f32),
            pltpu.VMEM((F, F), f32),
            pltpu.VMEM((2, configs, F), f32),
            pltpu.VMEM((hi_n, configs, 2 * F), f32),
            pltpu.VMEM((lo_n, configs, 2 * F), f32),
            pltpu.VMEM((hi_n, configs // 2, 2 * F), f32),
            pltpu.VMEM((lo_n, configs // 2, 2 * F), f32),
            pltpu.VMEM((n_src, 8, 2 * F), f32),
            pltpu.SemaphoreType.DMA((n_src,)),
            pltpu.SemaphoreType.DMA((n_src,)),
            pltpu.SemaphoreType.DMA((n_inst,)),
            pltpu.SemaphoreType.DMA((n_inst,)),
            pltpu.SemaphoreType.DMA((2, hi_n)),
            pltpu.SemaphoreType.DMA((2, hi_n)),
            pltpu.SemaphoreType.DMA((2, lo_n)),
            pltpu.SemaphoreType.DMA((2, lo_n)),
            pltpu.SemaphoreType.DMA((n_src,)),
            pltpu.SemaphoreType.DMA((n_src,)),
        ],
        compiler_params=pltpu.CompilerParams(
            collective_id=0, has_side_effects=True, vmem_limit_bytes=60 * 1024 * 1024
        ),
        name="lanczos",
    )(
        observed,
        basis.T,
        taps,
        epoch_owner.reshape(1, epochs),
        epoch_source.reshape(1, epochs),
        epoch_config.reshape(1, epochs),
        epoch_counts.reshape(1, 1),
    )
    block = 512
    whole = pl.BlockSpec((KDEV, samples), lambda i: (0, 0))
    sol_c, walk_c, sol_h, walk_h = pl.pallas_call(
        functools.partial(spread_out, samples, coefs),
        grid=(SRC_DEV // block,),
        out_shape=(jax.ShapeDtypeStruct((coefs, SRC_DEV), f32),) * 2
        + (jax.ShapeDtypeStruct((KDEV, samples), f32),) * 2,
        in_specs=[pl.BlockSpec((slots, 2 * F), lambda i: (0, 0)), whole, whole],
        out_specs=(pl.BlockSpec((coefs, block), lambda i: (0, i)),) * 2 + (whole, whole),
        scratch_shapes=[pltpu.VMEM((4 * F, slots), bf16), pltpu.VMEM((slots, 128), bf16)],
        compiler_params=pltpu.CompilerParams(vmem_limit_bytes=60 * 1024 * 1024),
        name="spread_out",
    )(z, xh, wh)
    return (sol_c, sol_h.T, walk_c, walk_h.T)


def solution(mesh):
    placed = (
        P(None, ("src", "inst")),
        P(),
        P(),
        P(("src", "inst"), None),
        P(("src", "inst")),
        P(("src", "inst")),
        P(("src", "inst")),
    )
    return jax.shard_map(
        on_device,
        mesh=mesh,
        in_specs=placed,
        out_specs=(P(None, "src"), P(None, "inst"), P(None, "src"), P(None, "inst")),
        check_vma=False,
    )
```

```python
import functools

import jax
import jax.numpy as jnp
from jax import lax
from jax.experimental import pallas as pl
from jax.experimental.pallas import tpu as pltpu
from jax.sharding import PartitionSpec as P

SRC_DEV = 4096
KDEV = 16
F = 64
MESH = pl.DeviceIdType.MESH
HIGHEST = lax.Precision.HIGHEST
f32, bf16 = jnp.float32, jnp.bfloat16


def iota(shape, dim):
    return lax.broadcasted_iota(jnp.int32, shape, dim)


def pieces(x, count):
    out = []
    for _ in range(count - 1):
        head = x.astype(bf16)
        out.append(head)
        x = x - head.astype(f32)
    out.append(x.astype(bf16))
    return out


def dot3(a, b):
    ah, al = pieces(a, 2)
    bh, bl = pieces(b, 2)
    return jnp.dot(
        jnp.concatenate([ah, al, ah], 1),
        jnp.concatenate([bh, bh, bl], 0),
        preferred_element_type=f32,
    )


def exact(a, b, dims=(((1,), (0,)), ((), ()))):
    return lax.dot_general(a, b, dims, precision=HIGHEST, preferred_element_type=f32)


def fold(onehot, x):
    width = x.shape[1]
    got = lax.dot_general(
        onehot, jnp.concatenate(pieces(x, 3), 1), (((0,), (0,)), ((), ())), preferred_element_type=f32
    )
    return got[:, :width] + got[:, width : 2 * width] + got[:, 2 * width :]


def total(x):
    return jnp.sum(x, axis=(0, 1), keepdims=True)


def stack8(x):
    return jnp.sum(x.reshape(x.shape[0] // 8, 8, x.shape[1]), axis=0)


def with_scalars(block, first, *values):
    lane, row = iota(block.shape, 1), iota(block.shape, 0)
    for at, value in enumerate(values):
        block = jnp.where((lane == first + at) & (row == 0), value, block)
    return block


def lanczos(
    dims,
    obs, basis_t, taps, owner, source, config, counts,
    v1_out, v2_out, v3_out, mix_out, xh_out, wh_out,
    send, recv, slots, quads, c0s, cgs, nss, counted, share, v2s, v3s, rpad, tables,
    match, zt, cols1, cols2, cols3, out_sem,
    a1, a2, b1, b2, norms,
    send_sem, recv_sem, fsend_sem, frecv_sem, xsend, xrecv, ysend, yrecv, nsend, nrecv,
):
    n_src, n_inst, rows, configs, hi_n, lo_n, chunk, sources = dims
    me, mine = lax.axis_index("src"), lax.axis_index("inst")
    my_hi, my_lo = me // lo_n, lax.rem(me, lo_n)
    samples, epochs = obs.shape
    coefs = basis_t.shape[0]
    half_rows = n_inst * n_src * rows
    steps = 2 * half_rows // chunk

    barrier = pltpu.get_barrier_semaphore()
    for step in range(1, n_src):
        pl.semaphore_signal(barrier, inc=1, device_id=(lax.rem(me + step, n_src), mine), device_id_type=MESH)
    for step in range(1, n_inst):
        pl.semaphore_signal(barrier, inc=1, device_id=(me, lax.rem(mine + step, n_inst)), device_id_type=MESH)

    own = owner[...]
    table = own == iota((n_src, epochs), 0)
    before = (iota((epochs, epochs), 0) < iota((epochs, epochs), 1)).astype(bf16)
    earlier = jnp.dot(table.astype(bf16), before, preferred_element_type=f32)
    slot = jnp.sum(jnp.where(table, earlier, 0.0), axis=0, keepdims=True).astype(jnp.int32)
    live = iota((1, epochs), 1) < counts[...]
    upper = slot >= rows
    place = jnp.where(live, own * rows + slot - jnp.where(upper, rows, 0), -1)
    hit = place == iota((n_src * rows, epochs), 0)
    data = jnp.concatenate(
        [
            obs[...],
            (source[...] + 1).astype(f32),
            config[...].astype(f32),
            jnp.ones((1, epochs), f32),
            jnp.zeros((F - samples - 3, epochs), f32),
        ],
        0,
    )
    stacked = jnp.concatenate(pieces(data, 3), 0)

    def packed(mask):
        got = lax.dot_general(
            mask.astype(bf16), stacked, (((1,), (1,)), ((), ())), preferred_element_type=f32
        )
        return got[:, :F] + got[:, F : 2 * F] + got[:, 2 * F :]

    send[...] = jnp.concatenate([packed(hit & ~upper), packed(hit & upper)], 1).reshape(n_src, rows, 2 * F)
    recv[mine, me] = send[me]

    pl.semaphore_wait(barrier, n_src + n_inst - 2)
    for step in range(1, n_src):
        peer = lax.rem(me + step, n_src)
        pltpu.make_async_remote_copy(
            send.at[peer], recv.at[mine, me], send_sem.at[peer], recv_sem.at[me],
            device_id=(peer, mine), device_id_type=MESH,
        ).start()

    spread = jnp.zeros((samples, samples), f32)
    offset = iota((samples, samples), 1) - iota((samples, samples), 0) + taps.shape[0] // 2
    for tap in range(taps.shape[0]):
        spread = jnp.where(offset == tap, taps[tap], spread)
    rpad[...] = jnp.zeros((F, F), f32)
    rpad[pl.ds(0, samples), pl.ds(0, coefs)] = exact(spread, basis_t[...], (((1,), (1,)), ((), ())))
    resp = rpad[...]
    gram = exact(resp, resp, (((0,), (0,)), ((), ())))
    resp_t = resp.T
    cweight = 0.4 * (1.0 + 3.0 * iota((configs, 1), 0).astype(f32) / configs)

    for step in range(1, n_src):
        peer = lax.rem(me + step, n_src)
        pltpu.make_async_remote_copy(
            send.at[peer], recv.at[mine, peer], send_sem.at[peer], recv_sem.at[peer],
            device_id=(peer, mine), device_id_type=MESH,
        ).wait()
    forwards = []
    for step in range(1, n_inst):
        other = lax.rem(mine + step, n_inst)
        pltpu.make_async_remote_copy(
            recv.at[mine], recv.at[mine], fsend_sem.at[other], frecv_sem.at[mine],
            device_id=(me, other), device_id_type=MESH,
        ).start()
        forwards.append(
            pltpu.make_async_remote_copy(
                recv.at[mine], recv.at[other], fsend_sem.at[other], frecv_sem.at[other],
                device_id=(me, other), device_id_type=MESH,
            )
        )
    for forward in forwards:
        forward.wait()

    held = recv[...].reshape(half_rows, 2 * F)
    slots[pl.ds(0, half_rows), :] = held[:, :F]
    slots[pl.ds(half_rows, half_rows), :] = held[:, F:]
    pick = (iota((8, 2 * F), 1) == samples + F * iota((8, 2 * F), 0)).astype(bf16)
    names = sum(
        lax.dot_general(pick, piece, (((1,), (1,)), ((), ())), preferred_element_type=f32)
        for piece in pieces(held, 2)
    )
    id_row = jnp.concatenate([names[0:1], names[1:2]], 1)
    id_row = jnp.where(id_row > 0.5, id_row, -1.0)
    lane = iota((1, F), 1)

    def at(step):
        return pl.ds(pl.multiple_of(step * chunk, chunk), chunk)

    def config_table(part):
        return (
            (part[:, samples + 1 : samples + 2] == iota((chunk, configs), 1).astype(f32))
            & (part[:, samples + 2 : samples + 3] > 0.5)
        ).astype(bf16)

    def project(step, carry):
        part = slots[at(step), :]
        spectra = jnp.where(lane < samples, part, 0.0)
        quads[at(step), :] = jnp.concatenate(
            pieces(dot3(spectra, resp), 2)
            + [jnp.broadcast_to(part[:, samples + 2 : samples + 3], (chunk, F)).astype(bf16), config_table(part)],
            1,
        )
        return carry + stack8(spectra * spectra)

    none = jnp.zeros((8, F), f32)
    unroll = steps <= 4
    b_sq = total(lax.fori_loop(0, steps, project, none, unroll=unroll))

    def gather(step, carry):
        stats, c_sq, quad = carry
        part = slots[at(step), :]
        name = part[:, samples : samples + 1]
        same = jnp.where(name == id_row, 1.0, 0.0).astype(bf16)
        got = jnp.dot(same, quads[...], preferred_element_type=f32)
        c0 = got[:, :F] + got[:, F : 2 * F]
        count = got[:, 2 * F : 3 * F]
        weight = 1.0 / jnp.maximum(count, 1.0)
        cg = dot3(c0, gram)
        c0s[at(step), :] = c0
        cgs[at(step), :] = count * cg
        nss[at(step), :] = got[:, 3 * F :]
        counted[at(step), :] = count
        share[at(step), :] = weight
        stats = stats + fold(config_table(part), jnp.concatenate([part, c0], 1))
        return stats, c_sq + stack8(c0 * c0 * weight), quad + stack8(c0 * cg)

    stats, c_sq, quad = lax.fori_loop(
        0, steps, gather, (jnp.zeros((configs, 2 * F), f32), none, none), unroll=unroll
    )

    lanes = match.shape[1]
    block = 512

    def ready(value):
        flat = value.T
        head = flat.astype(bf16)
        zt[pl.ds(0, F), :] = head
        zt[pl.ds(F, F), :] = (flat - head.astype(f32)).astype(bf16)

    def deposit(cols, first, last):
        def one_block(at_block, carry):
            groups = [at_block * (block // lanes) + i for i in range(block // lanes)]
            hit = jnp.concatenate(
                [
                    jnp.where(match[...] == group.astype(f32).astype(bf16), 1.0, 0.0).astype(bf16)
                    for group in groups
                ],
                1,
            )
            got = jnp.dot(zt[...], hit, preferred_element_type=f32)
            cols[:, pl.ds(pl.multiple_of(at_block * block, block), block)] = (got[:F] + got[F:])[:coefs]
            return carry

        lax.fori_loop(first, last, one_block, 0)

    def emit(which, cols, out):
        return pltpu.make_async_copy(cols, out, out_sem.at[which])

    blocks = sources // block

    def prepare_first():
        name = slots[:, samples : samples + 1].astype(jnp.int32) - 1
        match[...] = jnp.where((name & (lanes - 1)) == iota(match.shape, 1), name // lanes, -1).astype(f32).astype(bf16)
        ready(c0s[...] * share[...])
        deposit(cols1, 0, blocks // 4)

    def prepare_second():
        ready(v2s[...] * share[...])
        deposit(cols2, 0, blocks // 2)

    def swap(which, value, one_buf, two_buf, work1, work2):
        one_buf[my_hi] = value
        sent = []
        for step in range(1, hi_n):
            peer = lax.rem(my_hi + step, hi_n)
            pltpu.make_async_remote_copy(
                one_buf.at[my_hi], one_buf.at[my_hi], xsend.at[which, peer], xrecv.at[which, my_hi],
                device_id=(peer * lo_n + my_lo, mine), device_id_type=MESH,
            ).start()
            sent.append(pltpu.make_async_remote_copy(
                one_buf.at[my_hi], one_buf.at[peer], xsend.at[which, peer], xrecv.at[which, peer],
                device_id=(peer * lo_n + my_lo, mine), device_id_type=MESH,
            ))
        work1()
        for copy in sent:
            copy.wait()
        two_buf[my_lo] = jnp.sum(one_buf[...], axis=0)
        sent = []
        for step in range(1, lo_n):
            peer = lax.rem(my_lo + step, lo_n)
            pltpu.make_async_remote_copy(
                two_buf.at[my_lo], two_buf.at[my_lo], ysend.at[which, peer], yrecv.at[which, my_lo],
                device_id=(my_hi * lo_n + peer, mine), device_id_type=MESH,
            ).start()
            sent.append(pltpu.make_async_remote_copy(
                two_buf.at[my_lo], two_buf.at[peer], ysend.at[which, peer], yrecv.at[which, peer],
                device_id=(my_hi * lo_n + peer, mine), device_id_type=MESH,
            ))
        work2()
        for copy in sent:
            copy.wait()
        return jnp.sum(two_buf[...], axis=0)

    spare = 2 * F - 4
    got = swap(0, with_scalars(stats, spare, b_sq, total(c_sq), total(quad)), a1, a2,
               prepare_first, lambda: deposit(cols1, blocks // 4, blocks))
    emit(0, cols1, v1_out).start()
    b_sq, c_sq, quad = [got[0:1, spare + i : spare + i + 1] for i in range(3)]
    per_config = got[:configs, samples + 2 : samples + 3]
    h0 = jnp.where(lane < samples, got[:configs, :F], 0.0) * cweight
    p_sq = c_sq + total(h0 * h0)
    inv_p = 1.0 / jnp.sqrt(p_sq)
    beta1 = jnp.sqrt(b_sq)
    alpha1 = jnp.sqrt(p_sq) / beta1

    def table_step(h, s):
        hr = dot3(cweight * h, resp)
        mh = cweight * (dot3(s, resp_t) + per_config * cweight * h)
        return hr, mh, total(hr * s) + total(h * mh)

    h1 = h0 * inv_p
    hr1, mh1, extra = table_step(h1, jnp.where(lane < coefs, got[:, F:], 0.0) * inv_p)
    diag1 = quad * inv_p * inv_p + extra
    beta2 = jnp.sqrt(diag1 - alpha1 * alpha1)

    def second(step, carry):
        stats, v_sq, quad = carry
        v2 = (cgs[at(step), :] - diag1 * c0s[at(step), :]) * inv_p + dot3(nss[at(step), :], hr1)
        vg = dot3(v2, gram)
        v2s[at(step), :] = v2
        cgs[at(step), :] = counted[at(step), :] * vg
        stats = stats + fold(quads[at(step), 3 * F :], v2)
        return stats, v_sq + stack8(v2 * v2 * share[at(step), :]), quad + stack8(v2 * vg)

    stats, v_sq, quad = lax.fori_loop(
        0, steps, second, (jnp.zeros((configs, F), f32), none, none), unroll=unroll
    )
    wide = jnp.concatenate([stats[: configs // 2], stats[configs // 2 :]], 1)
    got = swap(1, with_scalars(wide, spare, total(v_sq), total(quad)), b1, b2,
               prepare_second, lambda: deposit(cols2, blocks // 2, blocks))
    emit(1, cols2, v2_out).start()
    v_sq, quad = [got[0:1, spare + i : spare + i + 1] for i in range(2)]
    h2 = mh1 - diag1 * h1
    off_sq = v_sq + total(h2 * h2)
    off1 = jnp.sqrt(off_sq)
    inv1 = 1.0 / off1
    h2 = h2 * inv1
    s2 = jnp.where(lane < coefs, jnp.concatenate([got[:, :F], got[:, F:]], 0), 0.0) * inv1
    hr2, mh2, extra = table_step(h2, s2)
    diag2 = quad * inv1 * inv1 + extra
    alpha2 = off1 / beta2
    beta3 = jnp.sqrt(diag2 - alpha2 * alpha2)

    def third(step, v_sq):
        v3 = (
            (cgs[at(step), :] - diag2 * v2s[at(step), :]) * inv1
            - (off1 * inv_p) * c0s[at(step), :]
            + dot3(nss[at(step), :], hr2)
        )
        v3s[at(step), :] = v3
        return v_sq + stack8(v3 * v3 * share[at(step), :])

    v_sq = lax.fori_loop(0, steps, third, none, unroll=unroll)
    norms[me] = jnp.concatenate([v_sq, none], 1)
    sent = []
    for step in range(1, n_src):
        peer = lax.rem(me + step, n_src)
        pltpu.make_async_remote_copy(
            norms.at[me], norms.at[me], nsend.at[peer], nrecv.at[me],
            device_id=(peer, mine), device_id_type=MESH,
        ).start()
        sent.append(pltpu.make_async_remote_copy(
            norms.at[me], norms.at[peer], nsend.at[peer], nrecv.at[peer],
            device_id=(peer, mine), device_id_type=MESH,
        ))
    ready(v3s[...] * share[...])
    deposit(cols3, 0, blocks)
    emit(2, cols3, v3_out).start()
    for copy in sent:
        copy.wait()
    v_sq = total(jnp.sum(norms[...], axis=0))
    h3 = mh2 - diag2 * h2 - off1 * h1
    off2 = jnp.sqrt(v_sq + total(h3 * h3))
    inv2 = 1.0 / off2
    alpha3 = off2 / beta3

    rho1 = jnp.sqrt(alpha1 * alpha1 + beta2 * beta2)
    cos1, sin1 = alpha1 / rho1, beta2 / rho1
    turn1, rhobar = sin1 * alpha2 / rho1, -cos1 * alpha2
    move1, phibar = cos1 * beta1 / rho1, sin1 * beta1
    rho2 = jnp.sqrt(rhobar * rhobar + beta3 * beta3)
    cos2, sin2 = rhobar / rho2, beta3 / rho2
    turn2, move2 = sin2 * alpha3 / rho2, cos2 * phibar / rho2

    walk = h2 - turn1 * h1
    tables[0] = move1 * h1 + move2 * walk
    tables[1] = inv2 * h3 - turn2 * walk
    kept = configs // n_inst
    xh_out[...] = tables[0, pl.ds(pl.multiple_of(mine * kept, kept), kept), pl.ds(0, samples)]
    wh_out[...] = tables[1, pl.ds(pl.multiple_of(mine * kept, kept), kept), pl.ds(0, samples)]

    mixes = [
        (move1 - move2 * turn1) * inv_p,
        move2 * inv1,
        turn2 * turn1 * inv_p,
        -turn2 * inv1,
        inv2,
    ]
    row = iota((8, 2 * F), 0)
    mix = jnp.zeros((8, 2 * F), f32)
    for index, value in enumerate(mixes):
        mix = jnp.where(row == index, value, mix)
    mix_out[...] = mix
    emit(0, cols1, v1_out).wait()
    emit(1, cols2, v2_out).wait()
    emit(2, cols3, v3_out).wait()


def combine(mix_ref, v1_ref, v2_ref, v3_ref, xh_ref, wh_ref, x_ref, w_ref, xt_ref, wt_ref):
    @pl.when(pl.program_id(0) == 0)
    def _():
        xt_ref[...] = xh_ref[...]
        wt_ref[...] = wh_ref[...]

    mix = [mix_ref[pl.ds(i, 1), pl.ds(0, 1)] for i in range(5)]
    v1, v2 = v1_ref[...], v2_ref[...]
    x_ref[...] = mix[0] * v1 + mix[1] * v2
    w_ref[...] = mix[2] * v1 + mix[3] * v2 + mix[4] * v3_ref[...]


def on_device(observed, basis, taps, epoch_owner, epoch_source, epoch_config, epoch_counts):
    n_src, n_inst = lax.axis_size("src"), lax.axis_size("inst")
    samples, epochs = observed.shape
    coefs = basis.shape[1]
    cap = max(2, epochs * 3 // (2 * n_src))
    rows = -(-cap // 16) * 8
    configs = KDEV * n_inst
    lo_n = 1
    while lo_n * lo_n * 4 <= n_src:
        lo_n *= 2
    hi_n = n_src // lo_n
    slots = 2 * rows * n_src * n_inst
    chunk = 512
    dims = (n_src, n_inst, rows, configs, hi_n, lo_n, chunk, SRC_DEV)
    vmem, smem = pl.BlockSpec(memory_space=pltpu.VMEM), pl.BlockSpec(memory_space=pltpu.SMEM)
    columns = jax.ShapeDtypeStruct((coefs, SRC_DEV), f32)
    v1, v2, v3, mix, xh, wh = pl.pallas_call(
        functools.partial(lanczos, dims),
        out_shape=(
            columns,
            columns,
            columns,
            jax.ShapeDtypeStruct((8, 2 * F), f32),
            jax.ShapeDtypeStruct((KDEV, samples), f32),
            jax.ShapeDtypeStruct((KDEV, samples), f32),
        ),
        in_specs=[vmem, vmem, smem, vmem, vmem, vmem, vmem],
        out_specs=(pl.BlockSpec(memory_space=pl.ANY),) * 3 + (vmem,) * 3,
        scratch_shapes=[
            pltpu.VMEM((n_src, rows, 2 * F), f32),
            pltpu.VMEM((n_inst, n_src, rows, 2 * F), f32),
            pltpu.VMEM((slots, F), f32),
            pltpu.VMEM((slots, 3 * F + configs), bf16),
            pltpu.VMEM((slots, F), f32),
            pltpu.VMEM((slots, F), f32),
            pltpu.VMEM((slots, configs), f32),
            pltpu.VMEM((slots, F), f32),
            pltpu.VMEM((slots, F), f32),
            pltpu.VMEM((slots, F), f32),
            pltpu.VMEM((slots, F), f32),
            pltpu.VMEM((F, F), f32),
            pltpu.VMEM((2, configs, F), f32),
            pltpu.VMEM((slots, 128), bf16),
            pltpu.VMEM((2 * F, slots), bf16),
            pltpu.VMEM((coefs, SRC_DEV), f32),
            pltpu.VMEM((coefs, SRC_DEV), f32),
            pltpu.VMEM((coefs, SRC_DEV), f32),
            pltpu.SemaphoreType.DMA((3,)),
            pltpu.VMEM((hi_n, configs, 2 * F), f32),
            pltpu.VMEM((lo_n, configs, 2 * F), f32),
            pltpu.VMEM((hi_n, configs // 2, 2 * F), f32),
            pltpu.VMEM((lo_n, configs // 2, 2 * F), f32),
            pltpu.VMEM((n_src, 8, 2 * F), f32),
            pltpu.SemaphoreType.DMA((n_src,)),
            pltpu.SemaphoreType.DMA((n_src,)),
            pltpu.SemaphoreType.DMA((n_inst,)),
            pltpu.SemaphoreType.DMA((n_inst,)),
            pltpu.SemaphoreType.DMA((2, hi_n)),
            pltpu.SemaphoreType.DMA((2, hi_n)),
            pltpu.SemaphoreType.DMA((2, lo_n)),
            pltpu.SemaphoreType.DMA((2, lo_n)),
            pltpu.SemaphoreType.DMA((n_src,)),
            pltpu.SemaphoreType.DMA((n_src,)),
        ],
        compiler_params=pltpu.CompilerParams(
            collective_id=0, has_side_effects=True, vmem_limit_bytes=60 * 1024 * 1024
        ),
        name="lanczos",
    )(
        observed,
        basis.T,
        taps,
        epoch_owner.reshape(1, epochs),
        epoch_source.reshape(1, epochs),
        epoch_config.reshape(1, epochs),
        epoch_counts.reshape(1, 1),
    )
    block = SRC_DEV // 4
    whole = pl.BlockSpec((KDEV, samples), lambda i: (0, 0))
    part = pl.BlockSpec((coefs, block), lambda i: (0, i))
    sol_c, walk_c, sol_h, walk_h = pl.pallas_call(
        combine,
        grid=(SRC_DEV // block,),
        out_shape=(columns,) * 2 + (jax.ShapeDtypeStruct((KDEV, samples), f32),) * 2,
        in_specs=[pl.BlockSpec((8, 2 * F), lambda i: (0, 0)), part, part, part, whole, whole],
        out_specs=(part, part, whole, whole),
        compiler_params=pltpu.CompilerParams(vmem_limit_bytes=32 * 1024 * 1024),
        name="combine",
    )(mix, v1, v2, v3, xh, wh)
    return (sol_c, sol_h.T, walk_c, walk_h.T)


def solution(mesh):
    placed = (
        P(None, ("src", "inst")),
        P(),
        P(),
        P(("src", "inst"), None),
        P(("src", "inst")),
        P(("src", "inst")),
        P(("src", "inst")),
    )
    return jax.shard_map(
        on_device,
        mesh=mesh,
        in_specs=placed,
        out_specs=(P(None, "src"), P(None, "inst"), P(None, "src"), P(None, "inst")),
        check_vma=False,
    )
```

```python
import functools

import jax
import jax.numpy as jnp
from jax import lax
from jax.experimental import pallas as pl
from jax.experimental.pallas import tpu as pltpu
from jax.sharding import PartitionSpec as P

SRC_DEV = 4096
KDEV = 16
F = 64
MESH = pl.DeviceIdType.MESH
HIGHEST = lax.Precision.HIGHEST
f32, bf16 = jnp.float32, jnp.bfloat16


def iota(shape, dim):
    return lax.broadcasted_iota(jnp.int32, shape, dim)


def pieces(x, count):
    out = []
    for _ in range(count - 1):
        head = x.astype(bf16)
        out.append(head)
        x = x - head.astype(f32)
    out.append(x.astype(bf16))
    return out


def dot3(a, b):
    ah, al = pieces(a, 2)
    bh, bl = pieces(b, 2)
    return jnp.dot(
        jnp.concatenate([ah, al, ah], 1),
        jnp.concatenate([bh, bh, bl], 0),
        preferred_element_type=f32,
    )


def exact(a, b, dims=(((1,), (0,)), ((), ()))):
    return lax.dot_general(a, b, dims, precision=HIGHEST, preferred_element_type=f32)


def fold(onehot, x):
    width = x.shape[1]
    got = lax.dot_general(
        onehot, jnp.concatenate(pieces(x, 3), 1), (((0,), (0,)), ((), ())), preferred_element_type=f32
    )
    return got[:, :width] + got[:, width : 2 * width] + got[:, 2 * width :]


def total(x):
    return jnp.sum(x, axis=(0, 1), keepdims=True)


def stack8(x):
    return jnp.sum(x.reshape(x.shape[0] // 8, 8, x.shape[1]), axis=0)


def with_scalars(block, first, *values):
    lane, row = iota(block.shape, 1), iota(block.shape, 0)
    for at, value in enumerate(values):
        block = jnp.where((lane == first + at) & (row == 0), value, block)
    return block


def lanczos(
    dims,
    obs, basis_t, taps, owner, source, config, counts,
    v1_out, v2_out, v3_out, mix_out, xh_out, wh_out,
    send, recv, slots, quads, c0s, cgs, nss, rpad, tables,
    match, zt, cols1, cols2, cols3, grams, counts_c, named_c, out_sem,
    a1, a2, b1, b2, norms,
    send_sem, recv_sem, fsend_sem, frecv_sem, xsend, xrecv, ysend, yrecv, nsend, nrecv,
):
    n_src, n_inst, rows, configs, hi_n, lo_n, chunk, sources = dims
    me, mine = lax.axis_index("src"), lax.axis_index("inst")
    my_hi, my_lo = me // lo_n, lax.rem(me, lo_n)
    samples, epochs = obs.shape
    coefs = basis_t.shape[0]
    half_rows = n_inst * n_src * rows
    steps = 2 * half_rows // chunk

    barrier = pltpu.get_barrier_semaphore()
    for step in range(1, n_src):
        pl.semaphore_signal(barrier, inc=1, device_id=(lax.rem(me + step, n_src), mine), device_id_type=MESH)
    for step in range(1, n_inst):
        pl.semaphore_signal(barrier, inc=1, device_id=(me, lax.rem(mine + step, n_inst)), device_id_type=MESH)

    own = owner[...]
    table = own == iota((n_src, epochs), 0)
    before = (iota((epochs, epochs), 0) < iota((epochs, epochs), 1)).astype(bf16)
    earlier = jnp.dot(table.astype(bf16), before, preferred_element_type=f32)
    slot = jnp.sum(jnp.where(table, earlier, 0.0), axis=0, keepdims=True).astype(jnp.int32)
    live = iota((1, epochs), 1) < counts[...]
    upper = slot >= rows
    place = jnp.where(live, own * rows + slot - jnp.where(upper, rows, 0), -1)
    hit = place == iota((n_src * rows, epochs), 0)
    data = jnp.concatenate(
        [
            obs[...],
            (source[...] + 1).astype(f32),
            config[...].astype(f32),
            jnp.ones((1, epochs), f32),
            jnp.zeros((F - samples - 3, epochs), f32),
        ],
        0,
    )
    stacked = jnp.concatenate(pieces(data, 3), 0)

    def packed(mask):
        got = lax.dot_general(
            mask.astype(bf16), stacked, (((1,), (1,)), ((), ())), preferred_element_type=f32
        )
        return got[:, :F] + got[:, F : 2 * F] + got[:, 2 * F :]

    send[...] = jnp.concatenate([packed(hit & ~upper), packed(hit & upper)], 1).reshape(n_src, rows, 2 * F)
    recv[mine, me] = send[me]

    pl.semaphore_wait(barrier, n_src + n_inst - 2)
    for step in range(1, n_src):
        peer = lax.rem(me + step, n_src)
        pltpu.make_async_remote_copy(
            send.at[peer], recv.at[mine, me], send_sem.at[peer], recv_sem.at[me],
            device_id=(peer, mine), device_id_type=MESH,
        ).start()

    spread = jnp.zeros((samples, samples), f32)
    offset = iota((samples, samples), 1) - iota((samples, samples), 0) + taps.shape[0] // 2
    for tap in range(taps.shape[0]):
        spread = jnp.where(offset == tap, taps[tap], spread)
    rpad[...] = jnp.zeros((F, F), f32)
    rpad[pl.ds(0, samples), pl.ds(0, coefs)] = exact(spread, basis_t[...], (((1,), (1,)), ((), ())))
    resp = rpad[...]
    gram = exact(resp, resp, (((0,), (0,)), ((), ())))
    resp_t = resp.T
    cweight = 0.4 * (1.0 + 3.0 * iota((configs, 1), 0).astype(f32) / configs)

    for step in range(1, n_src):
        peer = lax.rem(me + step, n_src)
        pltpu.make_async_remote_copy(
            send.at[peer], recv.at[mine, peer], send_sem.at[peer], recv_sem.at[peer],
            device_id=(peer, mine), device_id_type=MESH,
        ).wait()
    forwards = []
    for step in range(1, n_inst):
        other = lax.rem(mine + step, n_inst)
        pltpu.make_async_remote_copy(
            recv.at[mine], recv.at[mine], fsend_sem.at[other], frecv_sem.at[mine],
            device_id=(me, other), device_id_type=MESH,
        ).start()
        forwards.append(
            pltpu.make_async_remote_copy(
                recv.at[mine], recv.at[other], fsend_sem.at[other], frecv_sem.at[other],
                device_id=(me, other), device_id_type=MESH,
            )
        )
    for forward in forwards:
        forward.wait()

    held = recv[...].reshape(half_rows, 2 * F)
    slots[pl.ds(0, half_rows), :] = held[:, :F]
    slots[pl.ds(half_rows, half_rows), :] = held[:, F:]
    pick = (iota((8, 2 * F), 1) == samples + F * iota((8, 2 * F), 0)).astype(bf16)
    names = sum(
        lax.dot_general(pick, piece, (((1,), (1,)), ((), ())), preferred_element_type=f32)
        for piece in pieces(held, 2)
    )
    id_row = jnp.concatenate([names[0:1], names[1:2]], 1)
    id_row = jnp.where(id_row > 0.5, id_row, -1.0)
    lane = iota((1, F), 1)

    def at(step):
        return pl.ds(pl.multiple_of(step * chunk, chunk), chunk)

    def config_table(part):
        return (
            (part[:, samples + 1 : samples + 2] == iota((chunk, configs), 1).astype(f32))
            & (part[:, samples + 2 : samples + 3] > 0.5)
        ).astype(bf16)

    def project(step, carry):
        part = slots[at(step), :]
        spectra = jnp.where(lane < samples, part, 0.0)
        quads[at(step), :] = jnp.concatenate(
            pieces(dot3(spectra, resp), 2)
            + [jnp.broadcast_to(part[:, samples + 2 : samples + 3], (chunk, F)).astype(bf16), config_table(part)],
            1,
        )
        return carry + stack8(spectra * spectra)

    none = jnp.zeros((8, F), f32)
    unroll = steps <= 4
    b_sq = total(lax.fori_loop(0, steps, project, none, unroll=unroll))

    def gather(step, carry):
        stats, c_sq, quad = carry
        part = slots[at(step), :]
        name = part[:, samples : samples + 1]
        same = jnp.where(name == id_row, 1.0, 0.0).astype(bf16)
        got = jnp.dot(same, quads[...], preferred_element_type=f32)
        c0 = got[:, :F] + got[:, F : 2 * F]
        count = got[:, 2 * F : 3 * F]
        weight = 1.0 / jnp.maximum(count, 1.0)
        cg = dot3(c0, gram)
        c0s[at(step), :] = c0
        cgs[at(step), :] = count * cg
        nss[at(step), :] = got[:, 3 * F :]
        stats = stats + fold(config_table(part), jnp.concatenate([part, c0], 1))
        return stats, c_sq + stack8(c0 * c0 * weight), quad + stack8(c0 * cg)

    stats, c_sq, quad = lax.fori_loop(
        0, steps, gather, (jnp.zeros((configs, 2 * F), f32), none, none), unroll=unroll
    )

    lanes = match.shape[1]
    block = 512

    def here(at_block):
        return slice(None), pl.ds(pl.multiple_of(at_block * block, block), block)

    def deposit(at_block, carry):
        hit = jnp.concatenate(
            [
                jnp.where(
                    match[...] == (at_block * (block // lanes) + i).astype(f32).astype(bf16), 1.0, 0.0
                ).astype(bf16)
                for i in range(block // lanes)
            ],
            1,
        )
        got = jnp.dot(zt[...], hit, preferred_element_type=f32)
        c0 = got[:F] + got[F : 2 * F]
        cols1[here(at_block)] = c0
        counts_c[here(at_block)] = got[2 * F : 3 * F]
        named_c[here(at_block)] = got[3 * F :]
        grams[here(at_block)] = got[2 * F : 3 * F] * dot3(gram, c0)
        return carry

    def emit(which, cols, out):
        return pltpu.make_async_copy(cols, out, out_sem.at[which])

    blocks = sources // block

    def prepare_first():
        name = slots[:, samples : samples + 1].astype(jnp.int32) - 1
        match[...] = jnp.where((name & (lanes - 1)) == iota(match.shape, 1), name // lanes, -1).astype(f32).astype(bf16)
        zt[...] = quads[...].astype(f32).T.astype(bf16)
        lax.fori_loop(0, blocks // 4, deposit, 0)

    def finish_first():
        lax.fori_loop(blocks // 4, blocks, deposit, 0)

    def second_columns(first, last):
        hr1_t = hr1.T

        def one_block(at_block, carry):
            v2 = (grams[here(at_block)] - diag1 * cols1[here(at_block)]) * inv_p + dot3(hr1_t, named_c[here(at_block)])
            cols2[here(at_block)] = v2
            grams[here(at_block)] = counts_c[here(at_block)] * dot3(gram, v2)
            return carry

        lax.fori_loop(first, last, one_block, 0)

    def swap(which, value, one_buf, two_buf, work1, work2):
        one_buf[my_hi] = value
        sent = []
        for step in range(1, hi_n):
            peer = lax.rem(my_hi + step, hi_n)
            pltpu.make_async_remote_copy(
                one_buf.at[my_hi], one_buf.at[my_hi], xsend.at[which, peer], xrecv.at[which, my_hi],
                device_id=(peer * lo_n + my_lo, mine), device_id_type=MESH,
            ).start()
            sent.append(pltpu.make_async_remote_copy(
                one_buf.at[my_hi], one_buf.at[peer], xsend.at[which, peer], xrecv.at[which, peer],
                device_id=(peer * lo_n + my_lo, mine), device_id_type=MESH,
            ))
        work1()
        for copy in sent:
            copy.wait()
        two_buf[my_lo] = jnp.sum(one_buf[...], axis=0)
        sent = []
        for step in range(1, lo_n):
            peer = lax.rem(my_lo + step, lo_n)
            pltpu.make_async_remote_copy(
                two_buf.at[my_lo], two_buf.at[my_lo], ysend.at[which, peer], yrecv.at[which, my_lo],
                device_id=(my_hi * lo_n + peer, mine), device_id_type=MESH,
            ).start()
            sent.append(pltpu.make_async_remote_copy(
                two_buf.at[my_lo], two_buf.at[peer], ysend.at[which, peer], yrecv.at[which, peer],
                device_id=(my_hi * lo_n + peer, mine), device_id_type=MESH,
            ))
        work2()
        for copy in sent:
            copy.wait()
        return jnp.sum(two_buf[...], axis=0)

    spare = 2 * F - 4
    got = swap(0, with_scalars(stats, spare, b_sq, total(c_sq), total(quad)), a1, a2,
               prepare_first, finish_first)
    emit(0, cols1, v1_out).start()
    b_sq, c_sq, quad = [got[0:1, spare + i : spare + i + 1] for i in range(3)]
    per_config = got[:configs, samples + 2 : samples + 3]
    h0 = jnp.where(lane < samples, got[:configs, :F], 0.0) * cweight
    p_sq = c_sq + total(h0 * h0)
    inv_p = 1.0 / jnp.sqrt(p_sq)
    beta1 = jnp.sqrt(b_sq)
    alpha1 = jnp.sqrt(p_sq) / beta1

    def table_step(h, s):
        hr = dot3(cweight * h, resp)
        mh = cweight * (dot3(s, resp_t) + per_config * cweight * h)
        return hr, mh, total(hr * s) + total(h * mh)

    h1 = h0 * inv_p
    hr1, mh1, extra = table_step(h1, jnp.where(lane < coefs, got[:, F:], 0.0) * inv_p)
    diag1 = quad * inv_p * inv_p + extra
    beta2 = jnp.sqrt(diag1 - alpha1 * alpha1)

    def second(step, carry):
        stats, v_sq, quad = carry
        named = nss[at(step), :]
        weight = 1.0 / jnp.maximum(jnp.sum(named, axis=1, keepdims=True), 1.0)
        v2 = (cgs[at(step), :] - diag1 * c0s[at(step), :]) * inv_p + dot3(named, hr1)
        vg = dot3(v2, gram)
        stats = stats + fold(quads[at(step), 3 * F :], v2)
        return stats, v_sq + stack8(v2 * v2 * weight), quad + stack8(v2 * vg)

    stats, v_sq, quad = lax.fori_loop(
        0, steps, second, (jnp.zeros((configs, F), f32), none, none), unroll=unroll
    )
    wide = jnp.concatenate([stats[: configs // 2], stats[configs // 2 :]], 1)
    got = swap(1, with_scalars(wide, spare, total(v_sq), total(quad)), b1, b2,
               lambda: second_columns(0, blocks // 2), lambda: second_columns(blocks // 2, blocks))
    emit(1, cols2, v2_out).start()
    v_sq, quad = [got[0:1, spare + i : spare + i + 1] for i in range(2)]
    h2 = mh1 - diag1 * h1
    off_sq = v_sq + total(h2 * h2)
    off1 = jnp.sqrt(off_sq)
    inv1 = 1.0 / off1
    h2 = h2 * inv1
    s2 = jnp.where(lane < coefs, jnp.concatenate([got[:, :F], got[:, F:]], 0), 0.0) * inv1
    hr2, mh2, extra = table_step(h2, s2)
    diag2 = quad * inv1 * inv1 + extra
    alpha2 = off1 / beta2
    beta3 = jnp.sqrt(diag2 - alpha2 * alpha2)

    hr2_t = hr2.T

    def third(at_block, v_sq):
        v3 = (
            (grams[here(at_block)] - diag2 * cols2[here(at_block)]) * inv1
            - (off1 * inv_p) * cols1[here(at_block)]
            + dot3(hr2_t, named_c[here(at_block)])
        )
        cols3[here(at_block)] = v3
        square = stack8(v3 * v3)
        return v_sq + sum(square[:, i * lanes : (i + 1) * lanes] for i in range(block // lanes))

    v_sq = lax.fori_loop(0, blocks, third, jnp.zeros((8, lanes), f32))
    norms[me] = v_sq
    sent = []
    for step in range(1, n_src):
        peer = lax.rem(me + step, n_src)
        pltpu.make_async_remote_copy(
            norms.at[me], norms.at[me], nsend.at[peer], nrecv.at[me],
            device_id=(peer, mine), device_id_type=MESH,
        ).start()
        sent.append(pltpu.make_async_remote_copy(
            norms.at[me], norms.at[peer], nsend.at[peer], nrecv.at[peer],
            device_id=(peer, mine), device_id_type=MESH,
        ))
    emit(2, cols3, v3_out).start()
    for copy in sent:
        copy.wait()
    v_sq = total(jnp.sum(norms[...], axis=0))
    h3 = mh2 - diag2 * h2 - off1 * h1
    off2 = jnp.sqrt(v_sq + total(h3 * h3))
    inv2 = 1.0 / off2
    alpha3 = off2 / beta3

    rho1 = jnp.sqrt(alpha1 * alpha1 + beta2 * beta2)
    cos1, sin1 = alpha1 / rho1, beta2 / rho1
    turn1, rhobar = sin1 * alpha2 / rho1, -cos1 * alpha2
    move1, phibar = cos1 * beta1 / rho1, sin1 * beta1
    rho2 = jnp.sqrt(rhobar * rhobar + beta3 * beta3)
    cos2, sin2 = rhobar / rho2, beta3 / rho2
    turn2, move2 = sin2 * alpha3 / rho2, cos2 * phibar / rho2

    walk = h2 - turn1 * h1
    tables[0] = move1 * h1 + move2 * walk
    tables[1] = inv2 * h3 - turn2 * walk
    kept = configs // n_inst
    xh_out[...] = tables[0, pl.ds(pl.multiple_of(mine * kept, kept), kept), pl.ds(0, samples)]
    wh_out[...] = tables[1, pl.ds(pl.multiple_of(mine * kept, kept), kept), pl.ds(0, samples)]

    mixes = [
        (move1 - move2 * turn1) * inv_p,
        move2 * inv1,
        turn2 * turn1 * inv_p,
        -turn2 * inv1,
        inv2,
    ]
    row = iota((8, 2 * F), 0)
    mix = jnp.zeros((8, 2 * F), f32)
    for index, value in enumerate(mixes):
        mix = jnp.where(row == index, value, mix)
    mix_out[...] = mix
    emit(0, cols1, v1_out).wait()
    emit(1, cols2, v2_out).wait()
    emit(2, cols3, v3_out).wait()


def combine(mix_ref, v1_ref, v2_ref, v3_ref, xh_ref, wh_ref, x_ref, w_ref, xt_ref, wt_ref):
    @pl.when(pl.program_id(0) == 0)
    def _():
        xt_ref[...] = xh_ref[...]
        wt_ref[...] = wh_ref[...]

    mix = [mix_ref[pl.ds(i, 1), pl.ds(0, 1)] for i in range(5)]
    used = pl.ds(0, x_ref.shape[0])
    v1, v2 = v1_ref[used, :], v2_ref[used, :]
    x_ref[...] = mix[0] * v1 + mix[1] * v2
    w_ref[...] = mix[2] * v1 + mix[3] * v2 + mix[4] * v3_ref[used, :]


def on_device(observed, basis, taps, epoch_owner, epoch_source, epoch_config, epoch_counts):
    n_src, n_inst = lax.axis_size("src"), lax.axis_size("inst")
    samples, epochs = observed.shape
    coefs = basis.shape[1]
    cap = max(2, epochs * 3 // (2 * n_src))
    rows = -(-cap // 16) * 8
    configs = KDEV * n_inst
    lo_n = 1
    while lo_n * lo_n * 4 <= n_src:
        lo_n *= 2
    hi_n = n_src // lo_n
    slots = 2 * rows * n_src * n_inst
    chunk = 512
    dims = (n_src, n_inst, rows, configs, hi_n, lo_n, chunk, SRC_DEV)
    vmem, smem = pl.BlockSpec(memory_space=pltpu.VMEM), pl.BlockSpec(memory_space=pltpu.SMEM)
    columns = jax.ShapeDtypeStruct((F, SRC_DEV), f32)
    v1, v2, v3, mix, xh, wh = pl.pallas_call(
        functools.partial(lanczos, dims),
        out_shape=(
            columns,
            columns,
            columns,
            jax.ShapeDtypeStruct((8, 2 * F), f32),
            jax.ShapeDtypeStruct((KDEV, samples), f32),
            jax.ShapeDtypeStruct((KDEV, samples), f32),
        ),
        in_specs=[vmem, vmem, smem, vmem, vmem, vmem, vmem],
        out_specs=(pl.BlockSpec(memory_space=pl.ANY),) * 3 + (vmem,) * 3,
        scratch_shapes=[
            pltpu.VMEM((n_src, rows, 2 * F), f32),
            pltpu.VMEM((n_inst, n_src, rows, 2 * F), f32),
            pltpu.VMEM((slots, F), f32),
            pltpu.VMEM((slots, 3 * F + configs), bf16),
            pltpu.VMEM((slots, F), f32),
            pltpu.VMEM((slots, F), f32),
            pltpu.VMEM((slots, configs), f32),
            pltpu.VMEM((F, F), f32),
            pltpu.VMEM((2, configs, F), f32),
            pltpu.VMEM((slots, 128), bf16),
            pltpu.VMEM((3 * F + configs, slots), bf16),
            pltpu.VMEM((F, SRC_DEV), f32),
            pltpu.VMEM((F, SRC_DEV), f32),
            pltpu.VMEM((F, SRC_DEV), f32),
            pltpu.VMEM((F, SRC_DEV), f32),
            pltpu.VMEM((F, SRC_DEV), f32),
            pltpu.VMEM((configs, SRC_DEV), f32),
            pltpu.SemaphoreType.DMA((3,)),
            pltpu.VMEM((hi_n, configs, 2 * F), f32),
            pltpu.VMEM((lo_n, configs, 2 * F), f32),
            pltpu.VMEM((hi_n, configs // 2, 2 * F), f32),
            pltpu.VMEM((lo_n, configs // 2, 2 * F), f32),
            pltpu.VMEM((n_src, 8, 2 * F), f32),
            pltpu.SemaphoreType.DMA((n_src,)),
            pltpu.SemaphoreType.DMA((n_src,)),
            pltpu.SemaphoreType.DMA((n_inst,)),
            pltpu.SemaphoreType.DMA((n_inst,)),
            pltpu.SemaphoreType.DMA((2, hi_n)),
            pltpu.SemaphoreType.DMA((2, hi_n)),
            pltpu.SemaphoreType.DMA((2, lo_n)),
            pltpu.SemaphoreType.DMA((2, lo_n)),
            pltpu.SemaphoreType.DMA((n_src,)),
            pltpu.SemaphoreType.DMA((n_src,)),
        ],
        compiler_params=pltpu.CompilerParams(
            collective_id=0, has_side_effects=True, vmem_limit_bytes=60 * 1024 * 1024
        ),
        name="lanczos",
    )(
        observed,
        basis.T,
        taps,
        epoch_owner.reshape(1, epochs),
        epoch_source.reshape(1, epochs),
        epoch_config.reshape(1, epochs),
        epoch_counts.reshape(1, 1),
    )
    block = SRC_DEV // 4
    whole = pl.BlockSpec((KDEV, samples), lambda i: (0, 0))
    part = pl.BlockSpec((F, block), lambda i: (0, i))
    kept = pl.BlockSpec((coefs, block), lambda i: (0, i))
    sol_c, walk_c, sol_h, walk_h = pl.pallas_call(
        combine,
        grid=(SRC_DEV // block,),
        out_shape=(jax.ShapeDtypeStruct((coefs, SRC_DEV), f32),) * 2
        + (jax.ShapeDtypeStruct((KDEV, samples), f32),) * 2,
        in_specs=[pl.BlockSpec((8, 2 * F), lambda i: (0, 0)), part, part, part, whole, whole],
        out_specs=(kept, kept, whole, whole),
        compiler_params=pltpu.CompilerParams(vmem_limit_bytes=60 * 1024 * 1024),
        name="combine",
    )(mix, v1, v2, v3, xh, wh)
    return (sol_c, sol_h.T, walk_c, walk_h.T)


def solution(mesh):
    placed = (
        P(None, ("src", "inst")),
        P(),
        P(),
        P(("src", "inst"), None),
        P(("src", "inst")),
        P(("src", "inst")),
        P(("src", "inst")),
    )
    return jax.shard_map(
        on_device,
        mesh=mesh,
        in_specs=placed,
        out_specs=(P(None, "src"), P(None, "inst"), P(None, "src"), P(None, "inst")),
        check_vma=False,
    )
```

```python
import functools

import jax
import jax.numpy as jnp
from jax import lax
from jax.experimental import pallas as pl
from jax.experimental.pallas import tpu as pltpu
from jax.sharding import PartitionSpec as P

SRC_DEV = 4096
KDEV = 16
F = 64
MESH = pl.DeviceIdType.MESH
HIGHEST = lax.Precision.HIGHEST
f32, bf16 = jnp.float32, jnp.bfloat16


def iota(shape, dim):
    return lax.broadcasted_iota(jnp.int32, shape, dim)


def pieces(x, count):
    out = []
    for _ in range(count - 1):
        head = x.astype(bf16)
        out.append(head)
        x = x - head.astype(f32)
    out.append(x.astype(bf16))
    return out


def dot3(a, b):
    ah, al = pieces(a, 2)
    bh, bl = pieces(b, 2)
    return jnp.dot(
        jnp.concatenate([ah, al, ah], 1),
        jnp.concatenate([bh, bh, bl], 0),
        preferred_element_type=f32,
    )


def exact(a, b, dims=(((1,), (0,)), ((), ()))):
    return lax.dot_general(a, b, dims, precision=HIGHEST, preferred_element_type=f32)


def fold(onehot, x):
    width = x.shape[1]
    got = lax.dot_general(
        onehot, jnp.concatenate(pieces(x, 3), 1), (((0,), (0,)), ((), ())), preferred_element_type=f32
    )
    return got[:, :width] + got[:, width : 2 * width] + got[:, 2 * width :]


def total(x):
    return jnp.sum(x, axis=(0, 1), keepdims=True)


def stack8(x):
    return jnp.sum(x.reshape(x.shape[0] // 8, 8, x.shape[1]), axis=0)


def with_scalars(block, first, *values):
    lane, row = iota(block.shape, 1), iota(block.shape, 0)
    for at, value in enumerate(values):
        block = jnp.where((lane == first + at) & (row == 0), value, block)
    return block


def lanczos(
    dims,
    obs, basis_t, taps, owner, source, config, counts,
    v1_out, v2_out, v3_out, mix_out, xh_out, wh_out,
    send, recv, slots, quads, c0s, cgs, nss, rpad, tables,
    match, cols1, cols2, cols3, grams, counts_c, named_c, out_sem,
    a1, a2, b1, b2, norms,
    send_sem, recv_sem, fsend_sem, frecv_sem, xsend, xrecv, ysend, yrecv, nsend, nrecv,
):
    n_src, n_inst, rows, configs, hi_n, lo_n, chunk, sources = dims
    me, mine = lax.axis_index("src"), lax.axis_index("inst")
    my_hi, my_lo = me // lo_n, lax.rem(me, lo_n)
    samples, epochs = obs.shape
    coefs = basis_t.shape[0]
    half_rows = n_inst * n_src * rows
    steps = 2 * half_rows // chunk

    barrier = pltpu.get_barrier_semaphore()
    for step in range(1, n_src):
        pl.semaphore_signal(barrier, inc=1, device_id=(lax.rem(me + step, n_src), mine), device_id_type=MESH)
    for step in range(1, n_inst):
        pl.semaphore_signal(barrier, inc=1, device_id=(me, lax.rem(mine + step, n_inst)), device_id_type=MESH)

    own = owner[...]
    table = own == iota((n_src, epochs), 0)
    before = (iota((epochs, epochs), 0) < iota((epochs, epochs), 1)).astype(bf16)
    earlier = jnp.dot(table.astype(bf16), before, preferred_element_type=f32)
    slot = jnp.sum(jnp.where(table, earlier, 0.0), axis=0, keepdims=True).astype(jnp.int32)
    live = iota((1, epochs), 1) < counts[...]
    upper = slot >= rows
    place = jnp.where(live, own * rows + slot - jnp.where(upper, rows, 0), -1)
    hit = place == iota((n_src * rows, epochs), 0)
    data = jnp.concatenate(
        [
            obs[...],
            (source[...] + 1).astype(f32),
            config[...].astype(f32),
            jnp.ones((1, epochs), f32),
            jnp.zeros((F - samples - 3, epochs), f32),
        ],
        0,
    )
    stacked = jnp.concatenate(pieces(data, 3), 0)

    def packed(mask):
        got = lax.dot_general(
            mask.astype(bf16), stacked, (((1,), (1,)), ((), ())), preferred_element_type=f32
        )
        return got[:, :F] + got[:, F : 2 * F] + got[:, 2 * F :]

    send[...] = jnp.concatenate([packed(hit & ~upper), packed(hit & upper)], 1).reshape(n_src, rows, 2 * F)
    recv[mine, me] = send[me]

    pl.semaphore_wait(barrier, n_src + n_inst - 2)
    for step in range(1, n_src):
        peer = lax.rem(me + step, n_src)
        pltpu.make_async_remote_copy(
            send.at[peer], recv.at[mine, me], send_sem.at[peer], recv_sem.at[me],
            device_id=(peer, mine), device_id_type=MESH,
        ).start()

    spread = jnp.zeros((samples, samples), f32)
    offset = iota((samples, samples), 1) - iota((samples, samples), 0) + taps.shape[0] // 2
    for tap in range(taps.shape[0]):
        spread = jnp.where(offset == tap, taps[tap], spread)
    rpad[...] = jnp.zeros((F, F), f32)
    rpad[pl.ds(0, samples), pl.ds(0, coefs)] = exact(spread, basis_t[...], (((1,), (1,)), ((), ())))
    resp = rpad[...]
    gram = exact(resp, resp, (((0,), (0,)), ((), ())))
    resp_t = resp.T
    cweight = 0.4 * (1.0 + 3.0 * iota((configs, 1), 0).astype(f32) / configs)

    for step in range(1, n_src):
        peer = lax.rem(me + step, n_src)
        pltpu.make_async_remote_copy(
            send.at[peer], recv.at[mine, peer], send_sem.at[peer], recv_sem.at[peer],
            device_id=(peer, mine), device_id_type=MESH,
        ).wait()
    forwards = []
    for step in range(1, n_inst):
        other = lax.rem(mine + step, n_inst)
        pltpu.make_async_remote_copy(
            recv.at[mine], recv.at[mine], fsend_sem.at[other], frecv_sem.at[mine],
            device_id=(me, other), device_id_type=MESH,
        ).start()
        forwards.append(
            pltpu.make_async_remote_copy(
                recv.at[mine], recv.at[other], fsend_sem.at[other], frecv_sem.at[other],
                device_id=(me, other), device_id_type=MESH,
            )
        )
    for forward in forwards:
        forward.wait()

    held = recv[...].reshape(half_rows, 2 * F)
    slots[pl.ds(0, half_rows), :] = held[:, :F]
    slots[pl.ds(half_rows, half_rows), :] = held[:, F:]
    pick = (iota((8, 2 * F), 1) == samples + F * iota((8, 2 * F), 0)).astype(bf16)
    names = sum(
        lax.dot_general(pick, piece, (((1,), (1,)), ((), ())), preferred_element_type=f32)
        for piece in pieces(held, 2)
    )
    id_row = jnp.concatenate([names[0:1], names[1:2]], 1)
    id_row = jnp.where(id_row > 0.5, id_row, -1.0)
    lane = iota((1, F), 1)

    def at(step):
        return pl.ds(pl.multiple_of(step * chunk, chunk), chunk)

    def config_table(part):
        return (
            (part[:, samples + 1 : samples + 2] == iota((chunk, configs), 1).astype(f32))
            & (part[:, samples + 2 : samples + 3] > 0.5)
        ).astype(bf16)

    def project(step, carry):
        part = slots[at(step), :]
        spectra = jnp.where(lane < samples, part, 0.0)
        quads[at(step), :] = jnp.concatenate(
            pieces(dot3(spectra, resp), 2)
            + [jnp.broadcast_to(part[:, samples + 2 : samples + 3], (chunk, F)).astype(bf16), config_table(part)],
            1,
        )
        return carry + stack8(spectra * spectra)

    none = jnp.zeros((8, F), f32)
    unroll = steps <= 4
    b_sq = total(lax.fori_loop(0, steps, project, none, unroll=unroll))

    def gather(step, carry):
        stats, c_sq, quad = carry
        part = slots[at(step), :]
        name = part[:, samples : samples + 1]
        same = jnp.where(name == id_row, 1.0, 0.0).astype(bf16)
        got = jnp.dot(same, quads[...], preferred_element_type=f32)
        c0 = got[:, :F] + got[:, F : 2 * F]
        count = got[:, 2 * F : 3 * F]
        weight = 1.0 / jnp.maximum(count, 1.0)
        cg = dot3(c0, gram)
        c0s[at(step), :] = c0
        cgs[at(step), :] = count * cg
        nss[at(step), :] = got[:, 3 * F :]
        stats = stats + fold(config_table(part), jnp.concatenate([part, c0], 1))
        return stats, c_sq + stack8(c0 * c0 * weight), quad + stack8(c0 * cg)

    stats, c_sq, quad = lax.fori_loop(
        0, steps, gather, (jnp.zeros((configs, 2 * F), f32), none, none), unroll=unroll
    )

    lanes = match.shape[0]
    block = 512

    def here(at_block):
        return slice(None), pl.ds(pl.multiple_of(at_block * block, block), block)

    def deposit(at_block, carry):
        hit = jnp.concatenate(
            [
                jnp.where(
                    match[...] == (at_block * (block // lanes) + i).astype(f32).astype(bf16), 1.0, 0.0
                ).astype(bf16)
                for i in range(block // lanes)
            ],
            0,
        )
        got = jnp.dot(hit, quads[...], preferred_element_type=f32).T
        c0 = got[:F] + got[F : 2 * F]
        cols1[here(at_block)] = c0
        counts_c[here(at_block)] = got[2 * F : 3 * F]
        named_c[here(at_block)] = got[3 * F :]
        grams[here(at_block)] = got[2 * F : 3 * F] * dot3(gram, c0)
        return carry

    def emit(which, cols, out):
        return pltpu.make_async_copy(cols, out, out_sem.at[which])

    blocks = sources // block

    def prepare_first():
        name = id_row.astype(jnp.int32) - 1
        match[...] = jnp.where((name & (lanes - 1)) == iota(match.shape, 0), name // lanes, -1).astype(f32).astype(bf16)
        lax.fori_loop(0, blocks // 4, deposit, 0)

    def finish_first():
        lax.fori_loop(blocks // 4, blocks, deposit, 0)

    def second_columns(first, last):
        hr1_t = hr1.T

        def one_block(at_block, carry):
            v2 = (grams[here(at_block)] - diag1 * cols1[here(at_block)]) * inv_p + dot3(hr1_t, named_c[here(at_block)])
            cols2[here(at_block)] = v2
            grams[here(at_block)] = counts_c[here(at_block)] * dot3(gram, v2)
            return carry

        lax.fori_loop(first, last, one_block, 0)

    def swap(which, value, one_buf, two_buf, work1, work2):
        one_buf[my_hi] = value
        sent = []
        for step in range(1, hi_n):
            peer = lax.rem(my_hi + step, hi_n)
            pltpu.make_async_remote_copy(
                one_buf.at[my_hi], one_buf.at[my_hi], xsend.at[which, peer], xrecv.at[which, my_hi],
                device_id=(peer * lo_n + my_lo, mine), device_id_type=MESH,
            ).start()
            sent.append(pltpu.make_async_remote_copy(
                one_buf.at[my_hi], one_buf.at[peer], xsend.at[which, peer], xrecv.at[which, peer],
                device_id=(peer * lo_n + my_lo, mine), device_id_type=MESH,
            ))
        work1()
        for copy in sent:
            copy.wait()
        two_buf[my_lo] = jnp.sum(one_buf[...], axis=0)
        sent = []
        for step in range(1, lo_n):
            peer = lax.rem(my_lo + step, lo_n)
            pltpu.make_async_remote_copy(
                two_buf.at[my_lo], two_buf.at[my_lo], ysend.at[which, peer], yrecv.at[which, my_lo],
                device_id=(my_hi * lo_n + peer, mine), device_id_type=MESH,
            ).start()
            sent.append(pltpu.make_async_remote_copy(
                two_buf.at[my_lo], two_buf.at[peer], ysend.at[which, peer], yrecv.at[which, peer],
                device_id=(my_hi * lo_n + peer, mine), device_id_type=MESH,
            ))
        work2()
        for copy in sent:
            copy.wait()
        return jnp.sum(two_buf[...], axis=0)

    spare = 2 * F - 4
    got = swap(0, with_scalars(stats, spare, b_sq, total(c_sq), total(quad)), a1, a2,
               prepare_first, finish_first)
    emit(0, cols1, v1_out).start()
    b_sq, c_sq, quad = [got[0:1, spare + i : spare + i + 1] for i in range(3)]
    per_config = got[:configs, samples + 2 : samples + 3]
    h0 = jnp.where(lane < samples, got[:configs, :F], 0.0) * cweight
    p_sq = c_sq + total(h0 * h0)
    inv_p = 1.0 / jnp.sqrt(p_sq)
    beta1 = jnp.sqrt(b_sq)
    alpha1 = jnp.sqrt(p_sq) / beta1

    def table_step(h, s):
        hr = dot3(cweight * h, resp)
        mh = cweight * (dot3(s, resp_t) + per_config * cweight * h)
        return hr, mh, total(hr * s) + total(h * mh)

    h1 = h0 * inv_p
    hr1, mh1, extra = table_step(h1, jnp.where(lane < coefs, got[:, F:], 0.0) * inv_p)
    diag1 = quad * inv_p * inv_p + extra
    beta2 = jnp.sqrt(diag1 - alpha1 * alpha1)

    def second(step, carry):
        stats, v_sq, quad = carry
        named = nss[at(step), :]
        weight = 1.0 / jnp.maximum(jnp.sum(named, axis=1, keepdims=True), 1.0)
        v2 = (cgs[at(step), :] - diag1 * c0s[at(step), :]) * inv_p + dot3(named, hr1)
        vg = dot3(v2, gram)
        stats = stats + fold(quads[at(step), 3 * F :], v2)
        return stats, v_sq + stack8(v2 * v2 * weight), quad + stack8(v2 * vg)

    stats, v_sq, quad = lax.fori_loop(
        0, steps, second, (jnp.zeros((configs, F), f32), none, none), unroll=unroll
    )
    wide = jnp.concatenate([stats[: configs // 2], stats[configs // 2 :]], 1)
    got = swap(1, with_scalars(wide, spare, total(v_sq), total(quad)), b1, b2,
               lambda: second_columns(0, blocks // 2), lambda: second_columns(blocks // 2, blocks))
    emit(1, cols2, v2_out).start()
    v_sq, quad = [got[0:1, spare + i : spare + i + 1] for i in range(2)]
    h2 = mh1 - diag1 * h1
    off_sq = v_sq + total(h2 * h2)
    off1 = jnp.sqrt(off_sq)
    inv1 = 1.0 / off1
    h2 = h2 * inv1
    s2 = jnp.where(lane < coefs, jnp.concatenate([got[:, :F], got[:, F:]], 0), 0.0) * inv1
    hr2, mh2, extra = table_step(h2, s2)
    diag2 = quad * inv1 * inv1 + extra
    alpha2 = off1 / beta2
    beta3 = jnp.sqrt(diag2 - alpha2 * alpha2)

    hr2_t = hr2.T

    def third(at_block, v_sq):
        v3 = (
            (grams[here(at_block)] - diag2 * cols2[here(at_block)]) * inv1
            - (off1 * inv_p) * cols1[here(at_block)]
            + dot3(hr2_t, named_c[here(at_block)])
        )
        cols3[here(at_block)] = v3
        square = stack8(v3 * v3)
        return v_sq + sum(square[:, i * lanes : (i + 1) * lanes] for i in range(block // lanes))

    v_sq = lax.fori_loop(0, blocks, third, jnp.zeros((8, lanes), f32))
    norms[me] = v_sq
    sent = []
    for step in range(1, n_src):
        peer = lax.rem(me + step, n_src)
        pltpu.make_async_remote_copy(
            norms.at[me], norms.at[me], nsend.at[peer], nrecv.at[me],
            device_id=(peer, mine), device_id_type=MESH,
        ).start()
        sent.append(pltpu.make_async_remote_copy(
            norms.at[me], norms.at[peer], nsend.at[peer], nrecv.at[peer],
            device_id=(peer, mine), device_id_type=MESH,
        ))
    emit(2, cols3, v3_out).start()
    for copy in sent:
        copy.wait()
    v_sq = total(jnp.sum(norms[...], axis=0))
    h3 = mh2 - diag2 * h2 - off1 * h1
    off2 = jnp.sqrt(v_sq + total(h3 * h3))
    inv2 = 1.0 / off2
    alpha3 = off2 / beta3

    rho1 = jnp.sqrt(alpha1 * alpha1 + beta2 * beta2)
    cos1, sin1 = alpha1 / rho1, beta2 / rho1
    turn1, rhobar = sin1 * alpha2 / rho1, -cos1 * alpha2
    move1, phibar = cos1 * beta1 / rho1, sin1 * beta1
    rho2 = jnp.sqrt(rhobar * rhobar + beta3 * beta3)
    cos2, sin2 = rhobar / rho2, beta3 / rho2
    turn2, move2 = sin2 * alpha3 / rho2, cos2 * phibar / rho2

    walk = h2 - turn1 * h1
    tables[0] = move1 * h1 + move2 * walk
    tables[1] = inv2 * h3 - turn2 * walk
    kept = configs // n_inst
    xh_out[...] = tables[0, pl.ds(pl.multiple_of(mine * kept, kept), kept), pl.ds(0, samples)]
    wh_out[...] = tables[1, pl.ds(pl.multiple_of(mine * kept, kept), kept), pl.ds(0, samples)]

    mixes = [
        (move1 - move2 * turn1) * inv_p,
        move2 * inv1,
        turn2 * turn1 * inv_p,
        -turn2 * inv1,
        inv2,
    ]
    row = iota((8, 2 * F), 0)
    mix = jnp.zeros((8, 2 * F), f32)
    for index, value in enumerate(mixes):
        mix = jnp.where(row == index, value, mix)
    mix_out[...] = mix
    emit(0, cols1, v1_out).wait()
    emit(1, cols2, v2_out).wait()
    emit(2, cols3, v3_out).wait()


def combine(mix_ref, v1_ref, v2_ref, v3_ref, xh_ref, wh_ref, x_ref, w_ref, xt_ref, wt_ref):
    @pl.when(pl.program_id(0) == 0)
    def _():
        xt_ref[...] = xh_ref[...]
        wt_ref[...] = wh_ref[...]

    mix = [mix_ref[pl.ds(i, 1), pl.ds(0, 1)] for i in range(5)]
    used = pl.ds(0, x_ref.shape[0])
    v1, v2 = v1_ref[used, :], v2_ref[used, :]
    x_ref[...] = mix[0] * v1 + mix[1] * v2
    w_ref[...] = mix[2] * v1 + mix[3] * v2 + mix[4] * v3_ref[used, :]


def on_device(observed, basis, taps, epoch_owner, epoch_source, epoch_config, epoch_counts):
    n_src, n_inst = lax.axis_size("src"), lax.axis_size("inst")
    samples, epochs = observed.shape
    coefs = basis.shape[1]
    cap = max(2, epochs * 3 // (2 * n_src))
    rows = -(-cap // 16) * 8
    configs = KDEV * n_inst
    lo_n = 1
    while lo_n * lo_n * 4 <= n_src:
        lo_n *= 2
    hi_n = n_src // lo_n
    slots = 2 * rows * n_src * n_inst
    chunk = 512
    dims = (n_src, n_inst, rows, configs, hi_n, lo_n, chunk, SRC_DEV)
    vmem, smem = pl.BlockSpec(memory_space=pltpu.VMEM), pl.BlockSpec(memory_space=pltpu.SMEM)
    columns = jax.ShapeDtypeStruct((F, SRC_DEV), f32)
    v1, v2, v3, mix, xh, wh = pl.pallas_call(
        functools.partial(lanczos, dims),
        out_shape=(
            columns,
            columns,
            columns,
            jax.ShapeDtypeStruct((8, 2 * F), f32),
            jax.ShapeDtypeStruct((KDEV, samples), f32),
            jax.ShapeDtypeStruct((KDEV, samples), f32),
        ),
        in_specs=[vmem, vmem, smem, vmem, vmem, vmem, vmem],
        out_specs=(pl.BlockSpec(memory_space=pl.ANY),) * 3 + (vmem,) * 3,
        scratch_shapes=[
            pltpu.VMEM((n_src, rows, 2 * F), f32),
            pltpu.VMEM((n_inst, n_src, rows, 2 * F), f32),
            pltpu.VMEM((slots, F), f32),
            pltpu.VMEM((slots, 3 * F + configs), bf16),
            pltpu.VMEM((slots, F), f32),
            pltpu.VMEM((slots, F), f32),
            pltpu.VMEM((slots, configs), f32),
            pltpu.VMEM((F, F), f32),
            pltpu.VMEM((2, configs, F), f32),
            pltpu.VMEM((128, slots), bf16),
            pltpu.VMEM((F, SRC_DEV), f32),
            pltpu.VMEM((F, SRC_DEV), f32),
            pltpu.VMEM((F, SRC_DEV), f32),
            pltpu.VMEM((F, SRC_DEV), f32),
            pltpu.VMEM((F, SRC_DEV), f32),
            pltpu.VMEM((configs, SRC_DEV), f32),
            pltpu.SemaphoreType.DMA((3,)),
            pltpu.VMEM((hi_n, configs, 2 * F), f32),
            pltpu.VMEM((lo_n, configs, 2 * F), f32),
            pltpu.VMEM((hi_n, configs // 2, 2 * F), f32),
            pltpu.VMEM((lo_n, configs // 2, 2 * F), f32),
            pltpu.VMEM((n_src, 8, 2 * F), f32),
            pltpu.SemaphoreType.DMA((n_src,)),
            pltpu.SemaphoreType.DMA((n_src,)),
            pltpu.SemaphoreType.DMA((n_inst,)),
            pltpu.SemaphoreType.DMA((n_inst,)),
            pltpu.SemaphoreType.DMA((2, hi_n)),
            pltpu.SemaphoreType.DMA((2, hi_n)),
            pltpu.SemaphoreType.DMA((2, lo_n)),
            pltpu.SemaphoreType.DMA((2, lo_n)),
            pltpu.SemaphoreType.DMA((n_src,)),
            pltpu.SemaphoreType.DMA((n_src,)),
        ],
        compiler_params=pltpu.CompilerParams(
            collective_id=0, has_side_effects=True, vmem_limit_bytes=60 * 1024 * 1024
        ),
        name="lanczos",
    )(
        observed,
        basis.T,
        taps,
        epoch_owner.reshape(1, epochs),
        epoch_source.reshape(1, epochs),
        epoch_config.reshape(1, epochs),
        epoch_counts.reshape(1, 1),
    )
    block = SRC_DEV // 4
    whole = pl.BlockSpec((KDEV, samples), lambda i: (0, 0))
    part = pl.BlockSpec((F, block), lambda i: (0, i))
    kept = pl.BlockSpec((coefs, block), lambda i: (0, i))
    sol_c, walk_c, sol_h, walk_h = pl.pallas_call(
        combine,
        grid=(SRC_DEV // block,),
        out_shape=(jax.ShapeDtypeStruct((coefs, SRC_DEV), f32),) * 2
        + (jax.ShapeDtypeStruct((KDEV, samples), f32),) * 2,
        in_specs=[pl.BlockSpec((8, 2 * F), lambda i: (0, 0)), part, part, part, whole, whole],
        out_specs=(kept, kept, whole, whole),
        compiler_params=pltpu.CompilerParams(vmem_limit_bytes=60 * 1024 * 1024),
        name="combine",
    )(mix, v1, v2, v3, xh, wh)
    return (sol_c, sol_h.T, walk_c, walk_h.T)


def solution(mesh):
    placed = (
        P(None, ("src", "inst")),
        P(),
        P(),
        P(("src", "inst"), None),
        P(("src", "inst")),
        P(("src", "inst")),
        P(("src", "inst")),
    )
    return jax.shard_map(
        on_device,
        mesh=mesh,
        in_specs=placed,
        out_specs=(P(None, "src"), P(None, "inst"), P(None, "src"), P(None, "inst")),
        check_vma=False,
    )
```
